32 devices in a mesh: row: 8 (over y, x, core), col: 4 (over z).
Axes of the slice: x: 2, y: 2, z: 4, core: 2. Of those that a mesh axis runs over, the one named last changes fastest.
Arguments:
- kernel: float32 [1, 2048, 2, 1024], P(None, 'row', None, 'col'), may hold values from 0 to 1.5, as said below
Outputs:
- factored: float32 [1, 2048, 2, 1024], P(None, 'row', None, 'col')
The draws below stay inside these ranges and needn't reach their ends.
Inputs may be any that keep to these rules, and one draw needn't show every extreme that they name: kernel is symmetric and positive definite with all eigenvalues at least about 0.5 (up to float32 rounding of the draw); its entries lie between 0 and 1.5.
All inputs are finite; a program needn't handle non-finite values.
Results may differ from the reference program's by a relative error of at most 0.0003.
Values sent between devices are 32-bit elements; how exact they have to be, the bound alone decides.
No kernel may reach another device: no remote copies, remote signals or barrier semaphores. Data moves between devices by JAX's collectives and lax.ppermute only.
A program may use at most 64 MiB of HBM per device.

```python
import jax
import jax.numpy as jnp
from jax import lax

NB = 256
KBR = 1
PANELS = 3
FEAT = 256
ORDER = 2048
KBC = 2


def draw_kernel(key, part):
    points = jax.random.normal(key, (ORDER, FEAT), jnp.float32) / jnp.sqrt(jnp.float32(FEAT))
    squares = jnp.sum(points * points, axis=1)
    inner = jnp.dot(points, points.T, precision=lax.Precision.HIGHEST)
    dist = jnp.maximum(squares[:, None] + squares[None, :] - 2.0 * inner, 0.0)
    gauss = jnp.exp(-dist)
    gauss = 0.5 * (gauss + gauss.T)
    index = jnp.arange(ORDER, dtype=jnp.int32)
    matrix = jnp.where(index[:, None] == index[None, :], jnp.float32(1.5), gauss)
    return matrix.reshape(KBR, ORDER // KBR, KBC, ORDER // KBC)


def setup_inputs(seed: int = 0) -> dict:
    key_list = jax.random.split(jax.random.key(seed), 2)
    kernel = draw_kernel(jax.random.fold_in(key_list[1], 71), 0)
    return dict(kernel=kernel)


def reference(kernel):
    full = kernel.reshape(ORDER, ORDER)
    for step in range(PANELS):
        start = step * NB
        end = start + NB
        factor = jnp.linalg.cholesky(full[start:end, start:end])
        lower = lax.linalg.triangular_solve(factor, full[end:, start:end], left_side=False, lower=True, transpose_a=True)
        full = full.at[end:, end:].add(-jnp.dot(lower, lower.T, precision=lax.Precision.HIGHEST))
        full = full.at[start:end, start:end].set(factor)
        full = full.at[end:, start:end].set(lower)
        full = full.at[:start, start:end].set(jnp.float32(0.0))
    width = PANELS * NB
    full = full.at[:width, width:].set(jnp.float32(0.0))
    return full.reshape(KBR, ORDER // KBR, KBC, ORDER // KBC)
```

```python
import jax
import jax.numpy as jnp
from jax import lax
from jax.experimental import pallas as pl
from jax.experimental.pallas import tpu as pltpu
from jax.sharding import PartitionSpec as P

PANELS = 3
HALF = 128
GROUPS = HALF // 8
NN = (((1,), (0,)), ((), ()))
NT = (((1,), (1,)), ((), ()))


def lane_b(x, j):
    return jnp.broadcast_to(x[:, j:j + 1], (8, 128))


def sub_b(x, t):
    return jnp.broadcast_to(x[t:t + 1, :], x.shape)


def wide(x):
    return jnp.concatenate([x, x], axis=1)


def split(x):
    high = x.astype(jnp.bfloat16)
    low = (x - high.astype(jnp.float32)).astype(jnp.bfloat16)
    return high, low


def mm(a, b, dims):
    dot = lambda u, v: lax.dot_general(u, v, dims, preferred_element_type=jnp.float32)
    return dot(a[0], b[0]) + (dot(a[0], b[1]) + dot(a[1], b[0]))


def eliminate(rows, count):
    iota = lax.broadcasted_iota(jnp.int32, (8, 128), 0)
    rows = list(rows)
    out = []
    ahead = None
    for b in range(count):
        k = 8 * b
        cols = {g: [lane_b(rows[g], k + j) for j in range(8)] for g in range(b, count) if g > b or ahead is None}
        if ahead is not None:
            cols[b] = ahead
        ahead = None
        if b + 1 < count:
            ahead = [lane_b(rows[b + 1], k + 8 + j) for j in range(8)]
        da = jnp.ones((8, 128), jnp.float32)
        db = jnp.zeros((8, 128), jnp.float32)
        dc = jnp.ones((8, 128), jnp.float32)
        pp = jnp.zeros((8, 256), jnp.float32)
        for t in range(0, 8, 2):
            first = {j: sub_b(cols[b][j], t) for j in range(t, 8)}
            second = {j: sub_b(cols[b][j], t + 1) for j in range(t + 1, 8)}
            a, q, c = first[t], first[t + 1], second[t + 1]
            rd = 1.0 / (a * c - q * q)
            da = jnp.where((iota == t) | (iota == t + 1), a, da)
            db = jnp.where(iota == t + 1, q, db)
            dc = jnp.where(iota == t + 1, c, dc)
            p0, p1 = sub_b(rows[b], t), sub_b(rows[b], t + 1)
            pp = jnp.where(wide(iota == t + 1), p0, pp)
            for g in range(b, count):
                if g == b and t == 6:
                    continue
                c0, c1 = cols[g][t], cols[g][t + 1]
                n0, n1 = c0 * c - c1 * q, c1 * a - c0 * q
                if g == b:
                    n0 = jnp.where(iota > t + 1, n0, 0.0)
                    n1 = jnp.where(iota > t + 1, n1, 0.0)
                m0, m1 = n0 * rd, n1 * rd
                rows[g] = rows[g] - (wide(m0) * p0 + wide(m1) * p1)
                for j in range(t + 2, 8):
                    cols[g][j] = cols[g][j] - (m0 * first[j] + m1 * second[j])
                if g == b + 1:
                    for j in range(8):
                        ahead[j] = ahead[j] - (m0 * sub_b(c0, j) + m1 * sub_b(c1, j))
        odd = (iota % 2) == 1
        f = jnp.where(odd, db / da, 0.0)
        piv = jnp.where(odd, dc - db * f, da)
        out.append((rows[b] - wide(f) * pp) * wide(lax.rsqrt(piv)))
    return out


def factor_half(aug):
    rows = eliminate([aug[8 * g:8 * g + 8, :] for g in range(GROUPS)], GROUPS)
    for g in range(GROUPS):
        aug[8 * g:8 * g + 8, :] = rows[g]


def factor_panel(block, aug, inverse):
    r = lax.broadcasted_iota(jnp.int32, (HALF, HALF), 0)
    c = lax.broadcasted_iota(jnp.int32, (HALF, HALF), 1)
    eye = jnp.where(r == c, 1.0, 0.0).astype(jnp.float32)
    aug[:, :HALF] = block[:HALF, :HALF]
    aug[:, HALF:] = eye
    factor_half(aug)
    w0 = aug[:, HALF:]
    sw0 = split(w0)
    side = split(block[HALF:, :HALF])
    low = split(mm(side, sw0, NT))
    up = split(mm(sw0, side, NT))
    aug[:, :HALF] = block[HALF:, HALF:] - mm(low, up, NN)
    aug[:, HALF:] = eye
    factor_half(aug)
    w1 = aug[:, HALF:]
    corner = mm(split(w1), split(mm(low, sw0, NN)), NN)
    inverse[:HALF, :HALF] = w0
    inverse[:HALF, HALF:] = jnp.zeros((HALF, HALF), jnp.float32)
    inverse[HALF:, :HALF] = -corner
    inverse[HALF:, HALF:] = w1


def panels_kernel(place, mine_ref, other_ref, own_ref, *refs):
    n_side = len(refs) - 9
    side_refs = refs[:n_side]
    right_ref, top_ref, out_ref, lead, row, aug, inverse, block, work = refs[n_side:]
    p, c, n_col = place[0], place[1], place[2]
    core = lax.rem(p, 2)
    for b in range(6):
        lead[b, pl.ds(pl.multiple_of(core * HALF, HALF), HALF), :] = mine_ref[b]
        lead[b, pl.ds(pl.multiple_of((1 - core) * HALF, HALF), HALF), :] = other_ref[b]
    row[c] = own_ref[...]
    for d in range(n_side):
        row[lax.bitwise_xor(c, d + 1)] = side_refs[d][...]

    block[...] = lead[0]
    factor_panel(block, aug, inverse)
    w0 = split(inverse[...])
    s10, s20 = split(lead[1]), split(lead[3])
    l10, l20 = split(mm(s10, w0, NT)), split(mm(s20, w0, NT))
    u01, u02 = split(mm(w0, s10, NT)), split(mm(w0, s20, NT))
    block[...] = lead[2] - mm(l10, u01, NN)
    factor_panel(block, aug, inverse)
    w1 = split(inverse[...])
    s21 = split(lead[4] - mm(l20, u01, NN))
    l21, u12 = split(mm(s21, w1, NT)), split(mm(w1, s21, NT))
    block[...] = lead[5] - mm(l20, u02, NN) - mm(l21, u12, NN)
    factor_panel(block, aug, inverse)
    w2 = split(inverse[...])

    x0 = mm(split(row[0]), w0, NT)
    sx0 = split(x0)
    x1 = mm(split(row[1] - mm(sx0, u01, NN)), w1, NT)
    sx1 = split(x1)
    x2 = mm(split(row[2] - mm(sx0, u02, NN) - mm(sx1, u12, NN)), w2, NT)
    sx2 = split(x2)

    def schur(target, member):
        y0 = split(mm(w0, split(top_ref[0, :, member, :]), NN))
        y1 = split(mm(w1, split(top_ref[1, :, member, :] - mm(l10, y0, NN)), NN))
        y2 = split(mm(w2, split(top_ref[2, :, member, :] - mm(l20, y0, NN) - mm(l21, y1, NN)), NN))
        return target - (mm(sx0, y0, NN) + mm(sx1, y1, NN) + mm(sx2, y2, NN))

    r = lax.broadcasted_iota(jnp.int32, (2 * HALF, 2 * HALF), 0)
    q = lax.broadcasted_iota(jnp.int32, (2 * HALF, 2 * HALF), 1)
    keep = jnp.where(p > c, 1, 0)
    diagonal = jnp.where(p == c, 1, 0)
    mask = (keep + diagonal * jnp.where(r >= q, 1, 0)) > 0

    @pl.when(c < PANELS)
    def _():
        panel = jnp.where(c == 0, x0, jnp.where(c == 1, x1, x2))
        out_ref[0, :, 0, :] = jnp.where(mask, panel, 0.0)

    @pl.when((c >= PANELS) & (p >= PANELS))
    def _():
        out_ref[0, :, 0, :] = schur(own_ref[...], 0)

    @pl.when((c >= PANELS) & (p < PANELS))
    def _():
        out_ref[0, :, 0, :] = jnp.zeros((2 * HALF, 2 * HALF), jnp.float32)

    @pl.when(p >= PANELS)
    def _():
        out_ref[0, :, 1, :] = schur(right_ref[...], 1)

    @pl.when(p < PANELS)
    def _():
        out_ref[0, :, 1, :] = jnp.zeros((2 * HALF, 2 * HALF), jnp.float32)


def swap(value, axis, bit):
    n = lax.axis_size(axis)
    return lax.ppermute(value, axis, [(i, i ^ bit) for i in range(n)])


def shards(kernel):
    n_row = lax.axis_size("row")
    n_col = lax.axis_size("col")
    p = lax.axis_index("row")
    c = lax.axis_index("col")
    nb = kernel.shape[1]
    own = kernel[0, :, 0, :]
    right = kernel[0, :, 1, :]
    top = lax.all_gather(kernel[0], "row")

    side = [swap(own, "col", d) for d in range(1, n_col)]
    panel = []
    for k in range(PANELS):
        value = own
        for d in range(1, n_col):
            value = jnp.where(jnp.bitwise_xor(c, d) == k, side[d - 1], value)
        panel.append(value)
    panel = jnp.stack(panel)

    core, across, along = p & 1, (p >> 1) & 1, (p >> 2) & 1
    halves = panel.reshape(PANELS, 2, HALF, nb)
    kept = jnp.where(core == 0, halves[:, 0], halves[:, 1])
    given = jnp.where(core == 0, halves[:, 1], halves[:, 0])
    got = swap(given, "row", 1)
    even = jnp.where(core == 0, kept, got)
    odd = jnp.where(core == 0, got, kept)
    group = jnp.where(across == 0, jnp.stack([even[0], odd[0], odd[1]]), even)
    group_x = swap(group, "row", 2)
    group_y = swap(group, "row", 4)
    part_y = swap(group_x[:, :HALF // 2], "row", 4)
    part_x = swap(group_y[:, HALF // 2:], "row", 2)
    mine = jnp.where(along == 0, group, group_y)
    other = jnp.where(along == 0, group_x, jnp.concatenate([part_y, part_x], axis=1))
    lead = jnp.concatenate([jnp.where(across == 0, mine, other), jnp.where(across == 0, other, mine)])
    bit = 8
    while bit < n_row:
        came = swap(lead, "row", bit)
        lead = jnp.where((p & bit) == 0, lead, came)
        bit *= 2
    partner = swap(lead, "row", 1)

    place = jnp.stack([p, c, jnp.int32(n_col)]).astype(jnp.int32)
    f32 = jnp.float32
    vmem = pl.BlockSpec(memory_space=pltpu.VMEM)
    return pl.pallas_call(
        panels_kernel,
        grid=(1,),
        out_shape=jax.ShapeDtypeStruct(kernel.shape, f32),
        in_specs=[pl.BlockSpec(memory_space=pltpu.SMEM)] + [vmem] * (4 + len(side))
        + [pl.BlockSpec((PANELS, nb, 2, nb), lambda i: (0, 0, 0, 0))],
        out_specs=vmem,
        scratch_shapes=[
            pltpu.VMEM((6, nb, nb), f32),
            pltpu.VMEM((n_col, nb, nb), f32),
            pltpu.VMEM((HALF, nb), f32),
            pltpu.VMEM((nb, nb), f32),
            pltpu.VMEM((nb, nb), f32),
            pltpu.VMEM((nb, nb), f32),
        ],
        compiler_params=pltpu.CompilerParams(vmem_limit_bytes=48 * 1024 * 1024),
        name="panels",
    )(place, lead, partner, own, *side, right, top)


def solution(mesh):
    in_specs = (P(None, "row", None, "col"),)
    out_specs = P(None, "row", None, "col")
    return jax.shard_map(shards, mesh=mesh, in_specs=in_specs, out_specs=out_specs, check_vma=False)
```

```python
import jax
import jax.numpy as jnp
from jax import lax
from jax.experimental import pallas as pl
from jax.experimental.pallas import tpu as pltpu
from jax.sharding import PartitionSpec as P

PANELS = 3
HALF = 128
GROUPS = HALF // 8
NN = (((1,), (0,)), ((), ()))
NT = (((1,), (1,)), ((), ()))


def lane_b(x, j):
    return jnp.broadcast_to(x[:, j:j + 1], (8, 128))


def sub_b(x, t):
    return jnp.broadcast_to(x[t:t + 1, :], x.shape)


def wide(x):
    return jnp.concatenate([x, x], axis=1)


def split(x):
    high = x.astype(jnp.bfloat16)
    low = (x - high.astype(jnp.float32)).astype(jnp.bfloat16)
    return high, low


def mm(a, b, dims):
    dot = lambda u, v: lax.dot_general(u, v, dims, preferred_element_type=jnp.float32)
    return dot(a[0], b[0]) + (dot(a[0], b[1]) + dot(a[1], b[0]))


def eliminate(rows, count):
    iota = lax.broadcasted_iota(jnp.int32, (8, 128), 0)
    rows = list(rows)
    out = []
    ahead = None
    for b in range(count):
        k = 8 * b
        cols = {g: [lane_b(rows[g], k + j) for j in range(8)] for g in range(b, count) if g > b or ahead is None}
        if ahead is not None:
            cols[b] = ahead
        ahead = None
        if b + 1 < count:
            ahead = [lane_b(rows[b + 1], k + 8 + j) for j in range(8)]
        da = jnp.ones((8, 128), jnp.float32)
        db = jnp.zeros((8, 128), jnp.float32)
        dc = jnp.ones((8, 128), jnp.float32)
        pp = jnp.zeros((8, 256), jnp.float32)
        for t in range(0, 8, 2):
            first = {j: sub_b(cols[b][j], t) for j in range(t, 8)}
            second = {j: sub_b(cols[b][j], t + 1) for j in range(t + 1, 8)}
            a, q, c = first[t], first[t + 1], second[t + 1]
            rd = 1.0 / (a * c - q * q)
            da = jnp.where((iota == t) | (iota == t + 1), a, da)
            db = jnp.where(iota == t + 1, q, db)
            dc = jnp.where(iota == t + 1, c, dc)
            p0, p1 = sub_b(rows[b], t), sub_b(rows[b], t + 1)
            pp = jnp.where(wide(iota == t + 1), p0, pp)
            for g in range(b, count):
                if g == b and t == 6:
                    continue
                c0, c1 = cols[g][t], cols[g][t + 1]
                n0, n1 = c0 * c - c1 * q, c1 * a - c0 * q
                if g == b:
                    n0 = jnp.where(iota > t + 1, n0, 0.0)
                    n1 = jnp.where(iota > t + 1, n1, 0.0)
                m0, m1 = n0 * rd, n1 * rd
                rows[g] = rows[g] - (wide(m0) * p0 + wide(m1) * p1)
                for j in range(t + 2, 8):
                    cols[g][j] = cols[g][j] - (m0 * first[j] + m1 * second[j])
                if g == b + 1:
                    for j in range(8):
                        ahead[j] = ahead[j] - (m0 * sub_b(c0, j) + m1 * sub_b(c1, j))
        odd = (iota % 2) == 1
        f = jnp.where(odd, db / da, 0.0)
        piv = jnp.where(odd, dc - db * f, da)
        out.append((rows[b] - wide(f) * pp) * wide(lax.rsqrt(piv)))
    return out


def factor_half(aug):
    rows = eliminate([aug[8 * g:8 * g + 8, :] for g in range(GROUPS)], GROUPS)
    for g in range(GROUPS):
        aug[8 * g:8 * g + 8, :] = rows[g]


def identity(n):
    r = lax.broadcasted_iota(jnp.int32, (n, n), 0)
    c = lax.broadcasted_iota(jnp.int32, (n, n), 1)
    return jnp.where(r == c, 1.0, 0.0).astype(jnp.float32)


def factor_panel(block, aug, inverse):
    aug[:, :HALF] = block[:HALF, :HALF]
    aug[:, HALF:] = identity(HALF)
    inverse[:HALF, HALF:] = jnp.zeros((HALF, HALF), jnp.float32)

    @pl.loop(0, 2)
    def _(half):
        factor_half(aug)
        sw = split(aug[:, HALF:])

        @pl.when(half == 0)
        def _():
            side = split(block[HALF:, :HALF])
            low = split(mm(side, sw, NT))
            up = split(mm(sw, side, NT))
            inverse[:HALF, :HALF] = aug[:, HALF:]
            inverse[HALF:, :HALF] = mm(low, sw, NN)
            aug[:, :HALF] = block[HALF:, HALF:] - mm(low, up, NN)
            aug[:, HALF:] = identity(HALF)

        @pl.when(half == 1)
        def _():
            inverse[HALF:, :HALF] = -mm(sw, split(inverse[HALF:, :HALF]), NN)
            inverse[HALF:, HALF:] = aug[:, HALF:]


def panels_kernel(place, mine_ref, other_ref, own_ref, *refs):
    n_side = len(refs) - 12
    side_refs = refs[:n_side]
    right_ref, top_ref, top_other_ref, out_ref, lead, top, row, aug, inverses, lower, upper, block = refs[n_side:]
    p, c, n_col = place[0], place[1], place[2]
    core = lax.rem(p, 2)
    here = pl.ds(pl.multiple_of(core * HALF, HALF), HALF)
    there = pl.ds(pl.multiple_of((1 - core) * HALF, HALF), HALF)
    for b in range(6):
        lead[b, here, :] = mine_ref[b]
        lead[b, there, :] = other_ref[b]
        top[b, here, :] = top_ref[b]
        top[b, there, :] = top_other_ref[b]
    row[c] = own_ref[...]
    for d in range(n_side):
        row[lax.bitwise_xor(c, d + 1)] = side_refs[d][...]

    block[...] = lead[0]

    @pl.loop(0, PANELS)
    def _(k):
        factor_panel(block, aug, inverses.at[k])
        w = split(inverses[k])

        @pl.when(k == 0)
        def _():
            for i, b in enumerate((1, 3)):
                s = split(lead[b])
                lower[i] = mm(s, w, NT)
                upper[i] = mm(w, s, NT)
            block[...] = lead[2] - mm(split(lower[0]), split(upper[0]), NN)

        @pl.when(k == 1)
        def _():
            s = split(lead[4] - mm(split(lower[1]), split(upper[0]), NN))
            l21, u12 = mm(s, w, NT), mm(w, s, NT)
            lower[2] = l21
            upper[2] = u12
            block[...] = lead[5] - mm(split(lower[1]), split(upper[1]), NN) - mm(split(l21), split(u12), NN)

    w0, w1, w2 = [split(inverses[k]) for k in range(PANELS)]
    l10, l20, l21 = [split(lower[k]) for k in range(PANELS)]
    u01, u02, u12 = [split(upper[k]) for k in range(PANELS)]

    x0 = mm(split(row[0]), w0, NT)
    sx0 = split(x0)
    x1 = mm(split(row[1] - mm(sx0, u01, NN)), w1, NT)
    sx1 = split(x1)
    x2 = mm(split(row[2] - mm(sx0, u02, NN) - mm(sx1, u12, NN)), w2, NT)
    sx2 = split(x2)

    def schur(target, member):
        y0 = split(mm(w0, split(top[3 * member]), NN))
        y1 = split(mm(w1, split(top[3 * member + 1] - mm(l10, y0, NN)), NN))
        y2 = split(mm(w2, split(top[3 * member + 2] - mm(l20, y0, NN) - mm(l21, y1, NN)), NN))
        return target - (mm(sx0, y0, NN) + mm(sx1, y1, NN) + mm(sx2, y2, NN))

    r = lax.broadcasted_iota(jnp.int32, (2 * HALF, 2 * HALF), 0)
    q = lax.broadcasted_iota(jnp.int32, (2 * HALF, 2 * HALF), 1)
    keep = jnp.where(p > c, 1, 0)
    diagonal = jnp.where(p == c, 1, 0)
    mask = (keep + diagonal * jnp.where(r >= q, 1, 0)) > 0

    @pl.when(c < PANELS)
    def _():
        panel = jnp.where(c == 0, x0, jnp.where(c == 1, x1, x2))
        out_ref[0, :, 0, :] = jnp.where(mask, panel, 0.0)

    @pl.when((c >= PANELS) & (p >= PANELS))
    def _():
        out_ref[0, :, 0, :] = schur(own_ref[...], 0)

    @pl.when((c >= PANELS) & (p < PANELS))
    def _():
        out_ref[0, :, 0, :] = jnp.zeros((2 * HALF, 2 * HALF), jnp.float32)

    @pl.when(p >= PANELS)
    def _():
        out_ref[0, :, 1, :] = schur(right_ref[...], 1)

    @pl.when(p < PANELS)
    def _():
        out_ref[0, :, 1, :] = jnp.zeros((2 * HALF, 2 * HALF), jnp.float32)


def swap(value, axis, bit):
    n = lax.axis_size(axis)
    return lax.ppermute(value, axis, [(i, i ^ bit) for i in range(n)])


def spread(kept, given, pick, p, n_row):
    core, across, along = p & 1, (p >> 1) & 1, (p >> 2) & 1
    got = swap(given, "row", 1)
    group = pick(jnp.where(core == 0, kept, got), jnp.where(core == 0, got, kept), across)
    group_x = swap(group, "row", 2)
    group_y = swap(group, "row", 4)
    part_y = swap(group_x[:, :HALF // 2], "row", 4)
    part_x = swap(group_y[:, HALF // 2:], "row", 2)
    mine = jnp.where(along == 0, group, group_y)
    other = jnp.where(along == 0, group_x, jnp.concatenate([part_y, part_x], axis=1))
    first, second = jnp.where(across == 0, mine, other), jnp.where(across == 0, other, mine)
    bit = 8
    while bit < n_row:
        first = jnp.where((p & bit) == 0, first, swap(first, "row", bit))
        second = jnp.where((p & bit) == 0, second, swap(second, "row", bit))
        bit *= 2
    return first, second


def shards(kernel):
    n_row = lax.axis_size("row")
    n_col = lax.axis_size("col")
    p = lax.axis_index("row")
    c = lax.axis_index("col")
    nb = kernel.shape[1]
    own = kernel[0, :, 0, :]
    right = kernel[0, :, 1, :]
    core = p & 1

    def cut(blocks):
        halves = blocks.reshape(blocks.shape[0], 2, HALF, nb)
        return jnp.where(core == 0, halves[:, 0], halves[:, 1]), jnp.where(core == 0, halves[:, 1], halves[:, 0])

    kept, given = cut(jnp.stack([own, right]))
    first, second = spread(kept, given, lambda even, odd, across: jnp.stack([even[0], odd[0], even[1], odd[1]]), p, n_row)
    top = jnp.stack([first[0], first[1], second[0], first[2], first[3], second[2]])
    top_other = swap(top, "row", 1)

    side = [swap(own, "col", d) for d in range(1, n_col)]
    panel = []
    for k in range(PANELS):
        value = own
        for d in range(1, n_col):
            value = jnp.where(jnp.bitwise_xor(c, d) == k, side[d - 1], value)
        panel.append(value)

    kept, given = cut(jnp.stack(panel))
    first, second = spread(
        kept, given, lambda even, odd, across: jnp.where(across == 0, jnp.stack([even[0], odd[0], odd[1]]), even), p, n_row)
    lead = jnp.concatenate([first, second])
    lead_other = swap(lead, "row", 1)

    place = jnp.stack([p, c, jnp.int32(n_col)]).astype(jnp.int32)
    f32 = jnp.float32
    vmem = pl.BlockSpec(memory_space=pltpu.VMEM)
    return pl.pallas_call(
        panels_kernel,
        out_shape=jax.ShapeDtypeStruct(kernel.shape, f32),
        in_specs=[pl.BlockSpec(memory_space=pltpu.SMEM)] + [vmem] * (6 + len(side)),
        out_specs=vmem,
        scratch_shapes=[
            pltpu.VMEM((6, nb, nb), f32),
            pltpu.VMEM((6, nb, nb), f32),
            pltpu.VMEM((n_col, nb, nb), f32),
            pltpu.VMEM((HALF, nb), f32),
            pltpu.VMEM((PANELS, nb, nb), f32),
            pltpu.VMEM((PANELS, nb, nb), f32),
            pltpu.VMEM((PANELS, nb, nb), f32),
            pltpu.VMEM((nb, nb), f32),
        ],
        compiler_params=pltpu.CompilerParams(vmem_limit_bytes=48 * 1024 * 1024),
        name="panels",
    )(place, lead, lead_other, own, *side, right, top, top_other)


def solution(mesh):
    in_specs = (P(None, "row", None, "col"),)
    out_specs = P(None, "row", None, "col")
    return jax.shard_map(shards, mesh=mesh, in_specs=in_specs, out_specs=out_specs, check_vma=False)
```

```python
import jax
import jax.numpy as jnp
from jax import lax
from jax.experimental import pallas as pl
from jax.experimental.pallas import tpu as pltpu
from jax.sharding import PartitionSpec as P

PANELS = 3
HALF = 128
GROUPS = HALF // 8
NN = (((1,), (0,)), ((), ()))
NT = (((1,), (1,)), ((), ()))
TN = (((0,), (0,)), ((), ()))


def lane_b(x, j):
    return jnp.broadcast_to(x[:, j:j + 1], (8, 128))


def sub_b(x, t):
    return jnp.broadcast_to(x[t:t + 1, :], x.shape)


def wide(x):
    return jnp.concatenate([x, x], axis=1)


def split(x):
    high = x.astype(jnp.bfloat16)
    low = (x - high.astype(jnp.float32)).astype(jnp.bfloat16)
    return high, low


def mm(a, b, dims):
    dot = lambda u, v: lax.dot_general(u, v, dims, preferred_element_type=jnp.float32)
    return dot(a[0], b[0]) + (dot(a[0], b[1]) + dot(a[1], b[0]))


def eliminate(rows, shift):
    count = len(rows)
    iota = lax.broadcasted_iota(jnp.int32, (8, 128), 0)
    rows = list(rows)
    out = []
    ahead = None
    for b in range(count):
        k = shift + 8 * b
        cols = {g: [lane_b(rows[g], k + j) for j in range(8)] for g in range(b, count) if g > b or ahead is None}
        if ahead is not None:
            cols[b] = ahead
        ahead = None
        if b + 1 < count:
            ahead = [lane_b(rows[b + 1], k + 8 + j) for j in range(8)]
        da = jnp.ones((8, 128), jnp.float32)
        db = jnp.zeros((8, 128), jnp.float32)
        dc = jnp.ones((8, 128), jnp.float32)
        pp = jnp.zeros((8, 256), jnp.float32)
        for t in range(0, 8, 2):
            first = {j: sub_b(cols[b][j], t) for j in range(t, 8)}
            second = {j: sub_b(cols[b][j], t + 1) for j in range(t + 1, 8)}
            a, q, c = first[t], first[t + 1], second[t + 1]
            rd = 1.0 / (a * c - q * q)
            da = jnp.where((iota == t) | (iota == t + 1), a, da)
            db = jnp.where(iota == t + 1, q, db)
            dc = jnp.where(iota == t + 1, c, dc)
            p0, p1 = sub_b(rows[b], t), sub_b(rows[b], t + 1)
            pp = jnp.where(wide(iota == t + 1), p0, pp)
            for g in range(b, count):
                if g == b and t == 6:
                    continue
                c0, c1 = cols[g][t], cols[g][t + 1]
                n0, n1 = c0 * c - c1 * q, c1 * a - c0 * q
                if g == b:
                    n0 = jnp.where(iota > t + 1, n0, 0.0)
                    n1 = jnp.where(iota > t + 1, n1, 0.0)
                m0, m1 = n0 * rd, n1 * rd
                rows[g] = rows[g] - (wide(m0) * p0 + wide(m1) * p1)
                for j in range(t + 2, 8):
                    cols[g][j] = cols[g][j] - (m0 * first[j] + m1 * second[j])
                if g == b + 1:
                    for j in range(8):
                        ahead[j] = ahead[j] - (m0 * sub_b(c0, j) + m1 * sub_b(c1, j))
        odd = (iota % 2) == 1
        f = jnp.where(odd, db / da, 0.0)
        piv = jnp.where(odd, dc - db * f, da)
        out.append((rows[b] - wide(f) * pp) * wide(lax.rsqrt(piv)))
    return out


def factor_half(aug):
    half = GROUPS // 2
    upper = eliminate([aug[8 * g:8 * g + 8, :] for g in range(half)], 0)
    high, low = split(jnp.concatenate(upper, axis=0))
    left = jnp.concatenate([high[:, :HALF], high[:, :HALF], low[:, :HALF]], axis=0)
    right = jnp.concatenate([high, low, high], axis=0)
    update = lax.dot_general(left, right, TN, preferred_element_type=jnp.float32)
    under = eliminate(
        [aug[8 * g:8 * g + 8, :] - update[8 * g:8 * g + 8, :] for g in range(half, GROUPS)], HALF // 2)
    for g, value in enumerate(upper + under):
        aug[8 * g:8 * g + 8, :] = value


def identity(n):
    r = lax.broadcasted_iota(jnp.int32, (n, n), 0)
    c = lax.broadcasted_iota(jnp.int32, (n, n), 1)
    return jnp.where(r == c, 1.0, 0.0).astype(jnp.float32)


def factor_panel(block, aug, inverse):
    aug[:, :HALF] = block[:HALF, :HALF]
    aug[:, HALF:] = identity(HALF)
    inverse[:HALF, HALF:] = jnp.zeros((HALF, HALF), jnp.float32)

    @pl.loop(0, 2)
    def _(half):
        factor_half(aug)
        sw = split(aug[:, HALF:])

        @pl.when(half == 0)
        def _():
            side = split(block[HALF:, :HALF])
            low = split(mm(side, sw, NT))
            up = split(mm(sw, side, NT))
            inverse[:HALF, :HALF] = aug[:, HALF:]
            inverse[HALF:, :HALF] = mm(low, sw, NN)
            aug[:, :HALF] = block[HALF:, HALF:] - mm(low, up, NN)
            aug[:, HALF:] = identity(HALF)

        @pl.when(half == 1)
        def _():
            inverse[HALF:, :HALF] = -mm(sw, split(inverse[HALF:, :HALF]), NN)
            inverse[HALF:, HALF:] = aug[:, HALF:]


def halves(mine, other, core):
    a, b = mine[...], other[...]
    return jnp.concatenate([jnp.where(core == 0, a, b), jnp.where(core == 0, b, a)], axis=0)


def three(refs, core):
    near, far, near_other, far_other = refs
    return [
        jnp.where(core == 0, near[...], near_other[...]),
        jnp.where(core == 0, near_other[...], near[...]),
        jnp.where(core == 0, far[...], far_other[...]),
    ]


def panels_kernel(place, own_ref, right_ref, b0_ref, b1_ref, b2_ref, *refs):
    lead_refs, top_refs, out_ref = refs[:4], refs[4:8], refs[8]
    lead, aug, inverses, upper, block = refs[9:]
    p, c = place[0], place[1]
    core = lax.rem(p, 2)
    nb = 2 * HALF
    for b in range(6):
        k = b % 3
        mine, other = lead_refs[b // 3], lead_refs[2 + b // 3]
        lead[b] = halves(mine.at[k], other.at[k], core)
    block[...] = lead[0]

    @pl.loop(0, PANELS)
    def _(k):
        factor_panel(block, aug, inverses.at[k])
        w = split(inverses[k])

        @pl.when(k == 0)
        def _():
            u01 = mm(w, split(lead[1]), NT)
            upper[0] = u01
            block[...] = lead[2] - mm(split(u01), split(u01), TN)

        @pl.when(k == 1)
        def _():
            w0 = split(inverses[0])
            u02 = split(mm(w0, split(lead[3]), NT))
            s12 = lead[4].T - mm(split(upper[0]), u02, TN)
            u12 = mm(w, split(s12), NN)
            upper[1] = mm(w0, split(lead[3]), NT)
            upper[2] = u12
            block[...] = lead[5] - mm(u02, u02, TN) - mm(split(u12), split(u12), TN)

    w0, w1, w2 = [split(inverses[k]) for k in range(PANELS)]
    u01, u02, u12 = [split(upper[k]) for k in range(PANELS)]

    x0 = mm(split(b0_ref[...]), w0, NT)
    sx0 = split(x0)
    x1 = mm(split(b1_ref[...] - mm(sx0, u01, NN)), w1, NT)
    sx1 = split(x1)
    x2 = mm(split(b2_ref[...] - mm(sx0, u02, NN) - mm(sx1, u12, NN)), w2, NT)
    sx2 = split(x2)

    @pl.when(c < PANELS)
    def _():
        r = lax.broadcasted_iota(jnp.int32, (nb, nb), 0)
        q = lax.broadcasted_iota(jnp.int32, (nb, nb), 1)
        keep = jnp.where(p > c, 1, 0)
        diagonal = jnp.where(p == c, 1, 0)
        mask = (keep + diagonal * jnp.where(r >= q, 1, 0)) > 0
        panel = jnp.where(c == 0, x0, jnp.where(c == 1, x1, x2))
        out_ref[0, :, 0, :] = jnp.where(mask, panel, 0.0)

    actives = [(c >= PANELS) & (p >= PANELS), p >= PANELS]
    for member, (active, target) in enumerate(zip(actives, (own_ref, right_ref))):
        @pl.when(active)
        def _():
            first = (1 - member) * nb
            t0, t1, t2 = three([ref.at[first:first + nb] for ref in top_refs], core)
            y0 = split(mm(w0, split(t0), NN))
            y1 = split(mm(w1, split(t1 - mm(u01, y0, TN)), NN))
            y2 = split(mm(w2, split(t2 - mm(u02, y0, TN) - mm(u12, y1, TN)), NN))
            out_ref[0, :, member, :] = target[...] - (mm(sx0, y0, NN) + mm(sx1, y1, NN) + mm(sx2, y2, NN))

        @pl.when((p < PANELS) & (c >= PANELS * (1 - member)))
        def _():
            out_ref[0, :, member, :] = jnp.zeros((nb, nb), jnp.float32)


def swap(value, axis, bit):
    n = lax.axis_size(axis)
    return lax.ppermute(value, axis, [(i, i ^ bit) for i in range(n)])


def after(value, *others):
    return lax.optimization_barrier((value, *others))[0]


def launch(value):
    far = swap(value, "row", 6)
    return [value, swap(value, "row", 2), swap(value, "row", 4), far]


def land(came, p, *others):
    n_row = lax.axis_size("row")
    came = lax.optimization_barrier((*came, *others))
    q = (p >> 1) & 3

    def pick(d):
        return jnp.where(d == 0, came[0], jnp.where(d == 1, came[1], jnp.where(d == 2, came[2], came[3])))

    near, far = pick(q), pick(q ^ 1)
    bit = 8
    while bit < n_row:
        near = jnp.where((p & bit) == 0, near, swap(near, "row", bit))
        far = jnp.where((p & bit) == 0, far, swap(far, "row", bit))
        bit *= 2
    return near, far


def shards(kernel):
    n_col = lax.axis_size("col")
    p = lax.axis_index("row")
    c = lax.axis_index("col")
    nb = kernel.shape[1]
    core = p & 1
    f32 = jnp.float32
    own = kernel[0, :, 0, :]
    right = kernel[0, :, 1, :]

    side = [own] + [swap(own, "col", d) for d in range(1, n_col)]
    top = land(launch(jnp.concatenate([right, own])), p)

    blocks = []
    for k in range(PANELS):
        value = side[0]
        for d in range(1, n_col):
            value = jnp.where(jnp.bitwise_xor(c, d) == k, side[d], value)
        blocks.append(value)

    panel = after(jnp.stack(blocks), *top).reshape(PANELS, 2, HALF, nb)
    kept = jnp.where(core == 0, panel[:, 0], panel[:, 1])
    got = swap(jnp.where(core == 0, panel[:, 1], panel[:, 0]), "row", 1)
    even, odd = jnp.where(core == 0, kept, got), jnp.where(core == 0, got, kept)
    group = jnp.where((p >> 1) & 3 == 0, jnp.stack([even[0], odd[0], odd[1]]), even)
    lead = land(launch(group), p)

    place = jnp.stack([p, c]).astype(jnp.int32)
    operands = [
        own, right, *blocks,
        *lead, swap(lead[0], "row", 1), swap(lead[1], "row", 1),
        *top, swap(top[0], "row", 1), swap(top[1], "row", 1),
    ]
    vmem = pl.BlockSpec(memory_space=pltpu.VMEM)
    return pl.pallas_call(
        panels_kernel,
        out_shape=jax.ShapeDtypeStruct(kernel.shape, f32),
        in_specs=[pl.BlockSpec(memory_space=pltpu.SMEM)] + [vmem] * len(operands),
        out_specs=vmem,
        scratch_shapes=[
            pltpu.VMEM((6, nb, nb), f32),
            pltpu.VMEM((HALF, nb), f32),
            pltpu.VMEM((PANELS, nb, nb), f32),
            pltpu.VMEM((PANELS, nb, nb), f32),
            pltpu.VMEM((nb, nb), f32),
        ],
        compiler_params=pltpu.CompilerParams(vmem_limit_bytes=48 * 1024 * 1024),
        name="panels",
    )(place, *operands)


def solution(mesh):
    in_specs = (P(None, "row", None, "col"),)
    out_specs = P(None, "row", None, "col")
    return jax.shard_map(shards, mesh=mesh, in_specs=in_specs, out_specs=out_specs, check_vma=False)
```

```python
import jax
import jax.numpy as jnp
from jax import lax
from jax.experimental import pallas as pl
from jax.experimental.pallas import tpu as pltpu
from jax.sharding import PartitionSpec as P

PANELS = 3
HALF = 128
GROUPS = HALF // 8
NN = (((1,), (0,)), ((), ()))
NT = (((1,), (1,)), ((), ()))
TN = (((0,), (0,)), ((), ()))


def lane_b(x, j):
    return jnp.broadcast_to(x[:, j:j + 1], (8, 128))


def sub_b(x, t):
    return jnp.broadcast_to(x[t:t + 1, :], x.shape)


def wide(x):
    return jnp.concatenate([x, x], axis=1)


def split(x):
    high = x.astype(jnp.bfloat16)
    low = (x - high.astype(jnp.float32)).astype(jnp.bfloat16)
    return high, low


def mm(a, b, dims):
    dot = lambda u, v: lax.dot_general(u, v, dims, preferred_element_type=jnp.float32)
    return dot(a[0], b[0]) + (dot(a[0], b[1]) + dot(a[1], b[0]))


def eliminate(rows, shift):
    count = len(rows)
    iota = lax.broadcasted_iota(jnp.int32, (8, 128), 0)
    rows = list(rows)
    out = []
    ahead = None
    for b in range(count):
        k = shift + 8 * b
        cols = {g: [lane_b(rows[g], k + j) for j in range(8)] for g in range(b, count) if g > b or ahead is None}
        if ahead is not None:
            cols[b] = ahead
        ahead = None
        if b + 1 < count:
            ahead = [lane_b(rows[b + 1], k + 8 + j) for j in range(8)]
        da = jnp.ones((8, 128), jnp.float32)
        db = jnp.zeros((8, 128), jnp.float32)
        dc = jnp.ones((8, 128), jnp.float32)
        pp = jnp.zeros((8, 256), jnp.float32)
        for t in range(0, 8, 2):
            first = {j: sub_b(cols[b][j], t) for j in range(t, 8)}
            second = {j: sub_b(cols[b][j], t + 1) for j in range(t + 1, 8)}
            a, q, c = first[t], first[t + 1], second[t + 1]
            rd = 1.0 / (a * c - q * q)
            da = jnp.where((iota == t) | (iota == t + 1), a, da)
            db = jnp.where(iota == t + 1, q, db)
            dc = jnp.where(iota == t + 1, c, dc)
            p0, p1 = sub_b(rows[b], t), sub_b(rows[b], t + 1)
            pp = jnp.where(wide(iota == t + 1), p0, pp)
            for g in range(b, count):
                if g == b and t == 6:
                    continue
                c0, c1 = cols[g][t], cols[g][t + 1]
                n0, n1 = c0 * c - c1 * q, c1 * a - c0 * q
                if g == b:
                    n0 = jnp.where(iota > t + 1, n0, 0.0)
                    n1 = jnp.where(iota > t + 1, n1, 0.0)
                m0, m1 = n0 * rd, n1 * rd
                rows[g] = rows[g] - (wide(m0) * p0 + wide(m1) * p1)
                for j in range(t + 2, 8):
                    cols[g][j] = cols[g][j] - (m0 * first[j] + m1 * second[j])
                if g == b + 1:
                    for j in range(8):
                        ahead[j] = ahead[j] - (m0 * sub_b(c0, j) + m1 * sub_b(c1, j))
        odd = (iota % 2) == 1
        f = jnp.where(odd, db / da, 0.0)
        piv = jnp.where(odd, dc - db * f, da)
        out.append((rows[b] - wide(f) * pp) * wide(lax.rsqrt(piv)))
    return out


def factor_half(aug):
    half = GROUPS // 2
    upper = eliminate([aug[8 * g:8 * g + 8, :] for g in range(half)], 0)
    high, low = split(jnp.concatenate(upper, axis=0))
    left = jnp.concatenate([high[:, :HALF], high[:, :HALF], low[:, :HALF]], axis=0)
    right = jnp.concatenate([high, low, high], axis=0)
    update = lax.dot_general(left, right, TN, preferred_element_type=jnp.float32)
    under = eliminate(
        [aug[8 * g:8 * g + 8, :] - update[8 * g:8 * g + 8, :] for g in range(half, GROUPS)], HALF // 2)
    for g, value in enumerate(upper + under):
        aug[8 * g:8 * g + 8, :] = value


def identity(n):
    r = lax.broadcasted_iota(jnp.int32, (n, n), 0)
    c = lax.broadcasted_iota(jnp.int32, (n, n), 1)
    return jnp.where(r == c, 1.0, 0.0).astype(jnp.float32)


def factor_panel(block, aug, inverse):
    aug[:, :HALF] = block[:HALF, :HALF]
    aug[:, HALF:] = identity(HALF)
    inverse[:HALF, HALF:] = jnp.zeros((HALF, HALF), jnp.float32)

    @pl.loop(0, 2)
    def _(half):
        factor_half(aug)
        sw = split(aug[:, HALF:])

        @pl.when(half == 0)
        def _():
            side = split(block[HALF:, :HALF])
            low = split(mm(side, sw, NT))
            up = split(mm(sw, side, NT))
            inverse[:HALF, :HALF] = aug[:, HALF:]
            inverse[HALF:, :HALF] = mm(low, sw, NN)
            aug[:, :HALF] = block[HALF:, HALF:] - mm(low, up, NN)
            aug[:, HALF:] = identity(HALF)

        @pl.when(half == 1)
        def _():
            inverse[HALF:, :HALF] = -mm(sw, split(inverse[HALF:, :HALF]), NN)
            inverse[HALF:, HALF:] = aug[:, HALF:]


def halves(mine, other, core):
    a, b = mine[...], other[...]
    return jnp.concatenate([jnp.where(core == 0, a, b), jnp.where(core == 0, b, a)], axis=0)


def three(refs, core):
    near, far, near_other, far_other = refs
    return [
        jnp.where(core == 0, near[...], near_other[...]),
        jnp.where(core == 0, near_other[...], near[...]),
        jnp.where(core == 0, far[...], far_other[...]),
    ]


def first_kernel(place, mine_ref, other_ref, inverse_ref, block, aug):
    block[...] = halves(mine_ref.at[:HALF], other_ref.at[:HALF], lax.rem(place[0], 2))
    factor_panel(block, aug, inverse_ref)


def rest_kernel(place, w0_ref, *refs):
    pieces, inverses, upper, block, aug = (refs[:2], refs[2:4]), refs[4], refs[5], refs[6], refs[7]
    core = lax.rem(place[0], 2)

    def piece(group, k):
        mine, other = pieces[group]
        return halves(mine.at[k * HALF:(k + 1) * HALF], other.at[k * HALF:(k + 1) * HALF], core)

    w0 = split(w0_ref[...])
    u01 = mm(w0, split(piece(1, 0)), NN)
    upper[0] = u01
    su01 = split(u01)
    block[...] = piece(1, 1) - mm(su01, su01, TN)

    @pl.loop(0, 2)
    def _(k):
        factor_panel(block, aug, inverses.at[k])

        @pl.when(k == 0)
        def _():
            u02 = mm(w0, split(piece(0, 1)), NT)
            upper[1] = u02
            su02 = split(u02)
            s12 = split(piece(1, 2).T - mm(split(upper[0]), su02, TN))
            u12 = mm(split(inverses[0]), s12, NN)
            upper[2] = u12
            su12 = split(u12)
            block[...] = piece(1, 3) - mm(su02, su02, TN) - mm(su12, su12, TN)


def apply_kernel(place, own_ref, right_ref, b0_ref, b1_ref, b2_ref, w0_ref, inverses, upper, *refs):
    top_refs, out_ref = (refs[2:4], refs[:2]), refs[4]
    p, c = place[0], place[1]
    core = lax.rem(p, 2)
    nb = 2 * HALF
    w0, w1, w2 = [split(w) for w in (w0_ref[...], inverses[0], inverses[1])]
    u01, u02, u12 = [split(upper[k]) for k in range(PANELS)]

    x0 = mm(split(b0_ref[...]), w0, NT)
    sx0 = split(x0)
    x1 = mm(split(b1_ref[...] - mm(sx0, u01, NN)), w1, NT)
    sx1 = split(x1)
    x2 = mm(split(b2_ref[...] - mm(sx0, u02, NN) - mm(sx1, u12, NN)), w2, NT)
    sx2 = split(x2)
    row = tuple(jnp.concatenate(parts, axis=1) for parts in zip(sx0, sx1, sx2))

    @pl.when(c < PANELS)
    def _():
        r = lax.broadcasted_iota(jnp.int32, (nb, nb), 0)
        q = lax.broadcasted_iota(jnp.int32, (nb, nb), 1)
        keep = jnp.where(p > c, 1, 0)
        diagonal = jnp.where(p == c, 1, 0)
        mask = (keep + diagonal * jnp.where(r >= q, 1, 0)) > 0
        panel = jnp.where(c == 0, x0, jnp.where(c == 1, x1, x2))
        out_ref[0, :, 0, :] = jnp.where(mask, panel, 0.0)

    def remaining(members):
        tops = []
        for member in members:
            tops.append(three([ref.at[k:k + nb] for ref in top_refs[member] for k in (0, nb)], core))
        t0, t1, t2 = [jnp.concatenate(t, axis=1) for t in zip(*tops)]
        y0 = split(mm(w0, split(t0), NN))
        y1 = split(mm(w1, split(t1 - mm(u01, y0, TN)), NN))
        y2 = split(mm(w2, split(t2 - mm(u02, y0, TN) - mm(u12, y1, TN)), NN))
        column = tuple(jnp.concatenate(parts, axis=0) for parts in zip(y0, y1, y2))
        loss = mm(row, column, NN)
        for i, member in enumerate(members):
            out_ref[0, :, member, :] = (own_ref, right_ref)[member][...] - loss[:, i * nb:(i + 1) * nb]

    @pl.when((p >= PANELS) & (c >= PANELS))
    def _():
        remaining((0, 1))

    @pl.when((p >= PANELS) & (c < PANELS))
    def _():
        remaining((1,))

    @pl.when(p < PANELS)
    def _():
        out_ref[0, :, 1, :] = jnp.zeros((nb, nb), jnp.float32)

    @pl.when((p < PANELS) & (c >= PANELS))
    def _():
        out_ref[0, :, 0, :] = jnp.zeros((nb, nb), jnp.float32)


def swap(value, axis, bit):
    n = lax.axis_size(axis)
    return lax.ppermute(value, axis, [(i, i ^ bit) for i in range(n)])


def after(value, *others):
    return lax.optimization_barrier((value, *others))[0]


def launch(value):
    far = swap(value, "row", 6)
    return [value, swap(value, "row", 2), swap(value, "row", 4), far]


def land(came, p, *others):
    n_row = lax.axis_size("row")
    came = lax.optimization_barrier((*came, *others))
    q = (p >> 1) & 3

    def pick(d):
        return jnp.where(d == 0, came[0], jnp.where(d == 1, came[1], jnp.where(d == 2, came[2], came[3])))

    near, far = pick(q), pick(q ^ 1)
    bit = 8
    while bit < n_row:
        near = jnp.where((p & bit) == 0, near, swap(near, "row", bit))
        far = jnp.where((p & bit) == 0, far, swap(far, "row", bit))
        bit *= 2
    return near, far


def steps_right(s, n_col):
    return [(k + s, k + s + 1) for k in range(PANELS) if k + s + 1 < n_col]


def along_col(own, right_block, c):
    n_row, n_col = lax.axis_size("row"), lax.axis_size("col")
    direct = n_col == PANELS + 1
    right, left, chips = [], [], [right_block]
    value = back = own
    for s in range(n_col - 2):
        came = [lax.ppermute(value, "col", steps_right(s, n_col))]
        if s < PANELS - 1:
            pairs = [(r * n_col + k - s, r * n_col + k - s - 1) for r in range(n_row) for k in range(s + 1, PANELS)]
            if direct and s == 0:
                pairs += [(r * n_col, r * n_col + n_col - 1) for r in (0, 2)]
            came.append(lax.ppermute(back, ("row", "col"), pairs))
            if s == 0:
                came += [swap(right_block, "row", 2), swap(right_block, "row", 4)]
            if s == 1:
                came.append(swap(chips[2], "row", 2))
            value, back, *more = lax.optimization_barrier(tuple(came))
            left.append(back)
            chips += more
        else:
            value = came[0]
        right.append(value)

    def pick(k):
        value = own
        for s, came in enumerate(right):
            value = jnp.where(c == k + 1 + s, came, value)
        for s, came in enumerate(left):
            value = jnp.where(c == k - 1 - s, came, value)
        return value

    def start_last(*others):
        return lax.ppermute(after(value, *others), "col", steps_right(n_col - 2, n_col))

    def finish(came, *others):
        return jnp.where(c == n_col - 1, after(came, *others), pick(0))

    if direct:
        ahead = jnp.where(c == n_col - 1, left[0], pick(0))
    else:
        ahead = finish(start_last())
    return ahead, [None, pick(1), pick(2)], chips, start_last, finish


def shards(kernel):
    n_col = lax.axis_size("col")
    p = lax.axis_index("row")
    c = lax.axis_index("col")
    nb = kernel.shape[1]
    core = p & 1
    chip = (p >> 1) & 3
    f32 = jnp.float32
    own = kernel[0, :, 0, :]
    right = kernel[0, :, 1, :]
    place = jnp.stack([p, c]).astype(jnp.int32)
    smem = pl.BlockSpec(memory_space=pltpu.SMEM)
    vmem = pl.BlockSpec(memory_space=pltpu.VMEM)
    square = jax.ShapeDtypeStruct((nb, nb), f32)
    chain = [pltpu.VMEM((nb, nb), f32), pltpu.VMEM((HALF, nb), f32)]

    def call(body, name, outs, scratch, micros, *operands):
        return pl.pallas_call(
            body,
            out_shape=outs,
            in_specs=[smem] + [vmem] * len(operands),
            out_specs=jax.tree.map(lambda _: vmem, outs),
            scratch_shapes=scratch,
            compiler_params=pltpu.CompilerParams(vmem_limit_bytes=24 * 1024 * 1024),
            cost_estimate=pl.CostEstimate(flops=0, bytes_accessed=int(micros * 3.5e6), transcendentals=0),
            name=name,
        )(place, *operands)

    def cut(blocks):
        parts = blocks.reshape(-1, 2, HALF, nb)
        kept = jnp.where(core == 0, parts[:, 0], parts[:, 1])
        got = swap(jnp.where(core == 0, parts[:, 1], parts[:, 0]), "row", 1)
        return jnp.where(core == 0, kept, got), jnp.where(core == 0, got, kept)

    def cross(*values):
        mine = jnp.concatenate(values)
        return [mine, swap(mine, "row", 1)]

    ahead, blocks, top, start_last, finish = along_col(own, right, c)
    even, odd = cut(jnp.stack([ahead, blocks[1], blocks[2]]))
    one = launch(even[0])
    top = cross(*land(top, p))
    one = land(one, p, *top)
    two = launch(jnp.concatenate([even[1], jnp.where(chip == 0, odd[1], even[2])]))
    last = start_last(*one)
    one = cross(*one)
    w0 = call(first_kernel, "first", square, chain, 6.5, *one)
    blocks[0] = finish(last, w0)
    two = cross(*land(two, p, w0, blocks[0]))
    top_own = launch(after(own, w0))
    inverses, upper = call(
        rest_kernel, "rest",
        (jax.ShapeDtypeStruct((2, nb, nb), f32), jax.ShapeDtypeStruct((PANELS, nb, nb), f32)), chain, 15.0,
        w0, *one, *two)
    top_own = cross(*land(top_own, p, inverses))
    return call(
        apply_kernel, "apply", jax.ShapeDtypeStruct(kernel.shape, f32), [], 6.0,
        own, right, *blocks, w0, inverses, upper, *top, *top_own)


def solution(mesh):
    in_specs = (P(None, "row", None, "col"),)
    out_specs = P(None, "row", None, "col")
    return jax.shard_map(shards, mesh=mesh, in_specs=in_specs, out_specs=out_specs, check_vma=False)
```

```python
import jax
import jax.numpy as jnp
from jax import lax
from jax.experimental import pallas as pl
from jax.experimental.pallas import tpu as pltpu
from jax.sharding import PartitionSpec as P

PANELS = 3
HALF = 128
GROUPS = HALF // 8
NN = (((1,), (0,)), ((), ()))
NT = (((1,), (1,)), ((), ()))
TN = (((0,), (0,)), ((), ()))


def lane_b(x, j):
    return jnp.broadcast_to(x[:, j:j + 1], (8, 128))


def sub_b(x, t):
    return jnp.broadcast_to(x[t:t + 1, :], x.shape)


def wide(x):
    return jnp.concatenate([x, x], axis=1)


def split(x):
    high = x.astype(jnp.bfloat16)
    low = (x - high.astype(jnp.float32)).astype(jnp.bfloat16)
    return high, low


def mm(a, b, dims):
    dot = lambda u, v: lax.dot_general(u, v, dims, preferred_element_type=jnp.float32)
    return dot(a[0], b[0]) + (dot(a[0], b[1]) + dot(a[1], b[0]))


def eliminate(rows, shift):
    count = len(rows)
    iota = lax.broadcasted_iota(jnp.int32, (8, 128), 0)
    rows = list(rows)
    out = []
    ahead = None
    for b in range(count):
        k = shift + 8 * b
        cols = {g: [lane_b(rows[g], k + j) for j in range(8)] for g in range(b, count) if g > b or ahead is None}
        if ahead is not None:
            cols[b] = ahead
        ahead = None
        if b + 1 < count:
            ahead = [lane_b(rows[b + 1], k + 8 + j) for j in range(8)]
        da = jnp.ones((8, 128), jnp.float32)
        db = jnp.zeros((8, 128), jnp.float32)
        dc = jnp.ones((8, 128), jnp.float32)
        pp = jnp.zeros((8, 256), jnp.float32)
        for t in range(0, 8, 2):
            first = {j: sub_b(cols[b][j], t) for j in range(t, 8)}
            second = {j: sub_b(cols[b][j], t + 1) for j in range(t + 1, 8)}
            a, q, c = first[t], first[t + 1], second[t + 1]
            rd = 1.0 / (a * c - q * q)
            da = jnp.where((iota == t) | (iota == t + 1), a, da)
            db = jnp.where(iota == t + 1, q, db)
            dc = jnp.where(iota == t + 1, c, dc)
            p0, p1 = sub_b(rows[b], t), sub_b(rows[b], t + 1)
            pp = jnp.where(wide(iota == t + 1), p0, pp)
            for g in range(b, count):
                if g == b and t == 6:
                    continue
                c0, c1 = cols[g][t], cols[g][t + 1]
                n0, n1 = c0 * c - c1 * q, c1 * a - c0 * q
                if g == b:
                    n0 = jnp.where(iota > t + 1, n0, 0.0)
                    n1 = jnp.where(iota > t + 1, n1, 0.0)
                m0, m1 = n0 * rd, n1 * rd
                rows[g] = rows[g] - (wide(m0) * p0 + wide(m1) * p1)
                for j in range(t + 2, 8):
                    cols[g][j] = cols[g][j] - (m0 * first[j] + m1 * second[j])
                if g == b + 1:
                    for j in range(8):
                        ahead[j] = ahead[j] - (m0 * sub_b(c0, j) + m1 * sub_b(c1, j))
        odd = (iota % 2) == 1
        f = jnp.where(odd, db / da, 0.0)
        piv = jnp.where(odd, dc - db * f, da)
        out.append((rows[b] - wide(f) * pp) * wide(lax.rsqrt(piv)))
    return out


def factor_half(a):
    half = GROUPS // 2
    aug = jnp.concatenate([a, identity(HALF)], axis=1)
    upper = eliminate([aug[8 * g:8 * g + 8, :] for g in range(half)], 0)
    high, low = split(jnp.concatenate(upper, axis=0))
    left = jnp.concatenate([high[:, :HALF], high[:, :HALF], low[:, :HALF]], axis=0)
    right = jnp.concatenate([high, low, high], axis=0)
    update = lax.dot_general(left, right, TN, preferred_element_type=jnp.float32)
    under = eliminate(
        [aug[8 * g:8 * g + 8, :] - update[8 * g:8 * g + 8, :] for g in range(half, GROUPS)], HALF // 2)
    return jnp.concatenate(upper + under, axis=0)[:, HALF:]


def identity(n):
    r = lax.broadcasted_iota(jnp.int32, (n, n), 0)
    c = lax.broadcasted_iota(jnp.int32, (n, n), 1)
    return jnp.where(r == c, 1.0, 0.0).astype(jnp.float32)


def factor_panel(block, inverse):
    w0 = factor_half(block[:HALF, :HALF])
    sw0 = split(w0)
    side = split(block[HALF:, :HALF])
    low = split(mm(side, sw0, NT))
    w1 = factor_half(block[HALF:, HALF:] - mm(low, split(mm(sw0, side, NT)), NN))
    inverse[:HALF, :HALF] = w0
    inverse[:HALF, HALF:] = jnp.zeros((HALF, HALF), jnp.float32)
    inverse[HALF:, :HALF] = -mm(split(w1), split(mm(low, sw0, NN)), NN)
    inverse[HALF:, HALF:] = w1


def halves(mine, other, core):
    a, b = mine[...], other[...]
    return jnp.concatenate([jnp.where(core == 0, a, b), jnp.where(core == 0, b, a)], axis=0)


def three(refs, core):
    near, far, near_other, far_other = refs
    return [
        jnp.where(core == 0, near[...], near_other[...]),
        jnp.where(core == 0, near_other[...], near[...]),
        jnp.where(core == 0, far[...], far_other[...]),
    ]


def first_kernel(place, mine_ref, other_ref, inverse_ref, block):
    block[...] = halves(mine_ref.at[:HALF], other_ref.at[:HALF], lax.rem(place[0], 2))
    factor_panel(block, inverse_ref)


def rest_kernel(place, w0_ref, *refs):
    pieces, inverses, upper, block, later = (refs[:2], refs[2:4]), refs[4], refs[5], refs[6], refs[7]
    core = lax.rem(place[0], 2)

    def piece(group, k):
        mine, other = pieces[group]
        return halves(mine.at[k * HALF:(k + 1) * HALF], other.at[k * HALF:(k + 1) * HALF], core)

    w0 = split(w0_ref[...])
    u01 = mm(w0, split(piece(1, 0)), NN)
    u02 = mm(w0, split(piece(0, 1)), NT)
    upper[0] = u01
    upper[1] = u02
    su01, su02 = split(u01), split(u02)
    block[...] = piece(1, 1) - mm(su01, su01, TN)
    later[0] = piece(1, 2).T - mm(su01, su02, TN)
    later[1] = piece(1, 3) - mm(su02, su02, TN)

    @pl.loop(0, 2)
    def _(k):
        factor_panel(block, inverses.at[k])

        @pl.when(k == 0)
        def _():
            u12 = mm(split(inverses[0]), split(later[0]), NN)
            upper[2] = u12
            su12 = split(u12)
            block[...] = later[1] - mm(su12, su12, TN)


def apply_kernel(place, own_ref, right_ref, b0_ref, b1_ref, b2_ref, w0_ref, inverses, upper, *refs):
    top_refs, out_ref = (refs[2:4], refs[:2]), refs[4]
    p, c = place[0], place[1]
    core = lax.rem(p, 2)
    nb = 2 * HALF

    def blocks(members):
        w0, w1, w2 = [split(w) for w in (w0_ref[...], inverses[0], inverses[1])]
        u01, u02, u12 = [split(upper[k]) for k in range(PANELS)]
        x0 = mm(split(b0_ref[...]), w0, NT)
        if members:
            tops = [three([ref.at[k:k + nb] for ref in top_refs[member] for k in (0, nb)], core) for member in members]
            t0, t1, t2 = [jnp.concatenate(t, axis=1) for t in zip(*tops)]
            y0 = split(mm(w0, split(t0), NN))
        sx0 = split(x0)
        x1 = mm(split(b1_ref[...] - mm(sx0, u01, NN)), w1, NT)
        if members:
            y1 = split(mm(w1, split(t1 - mm(u01, y0, TN)), NN))
        sx1 = split(x1)
        x2 = mm(split(b2_ref[...] - mm(sx0, u02, NN) - mm(sx1, u12, NN)), w2, NT)
        if members:
            y2 = split(mm(w2, split(t2 - mm(u02, y0, TN) - mm(u12, y1, TN)), NN))
            row = tuple(jnp.concatenate(parts, axis=1) for parts in zip(sx0, sx1, split(x2)))
            column = tuple(jnp.concatenate(parts, axis=0) for parts in zip(y0, y1, y2))
            loss = mm(row, column, NN)
            for i, member in enumerate(members):
                out_ref[0, :, member, :] = (own_ref, right_ref)[member][...] - loss[:, i * nb:(i + 1) * nb]
        return x0, x1, x2

    def panel(x0, x1, x2):
        r = lax.broadcasted_iota(jnp.int32, (nb, nb), 0)
        q = lax.broadcasted_iota(jnp.int32, (nb, nb), 1)
        keep = jnp.where(p > c, 1, 0)
        diagonal = jnp.where(p == c, 1, 0)
        mask = (keep + diagonal * jnp.where(r >= q, 1, 0)) > 0
        value = jnp.where(c == 0, x0, jnp.where(c == 1, x1, x2))
        out_ref[0, :, 0, :] = jnp.where(mask, value, 0.0)

    @pl.when((p >= PANELS) & (c >= PANELS))
    def _():
        blocks((0, 1))

    @pl.when((p >= PANELS) & (c < PANELS))
    def _():
        panel(*blocks((1,)))

    @pl.when((p < PANELS) & (c < PANELS))
    def _():
        panel(*blocks(()))
        out_ref[0, :, 1, :] = jnp.zeros((nb, nb), jnp.float32)

    @pl.when((p < PANELS) & (c >= PANELS))
    def _():
        out_ref[0, :, 0, :] = jnp.zeros((nb, nb), jnp.float32)
        out_ref[0, :, 1, :] = jnp.zeros((nb, nb), jnp.float32)


def swap(value, axis, bit):
    n = lax.axis_size(axis)
    return lax.ppermute(value, axis, [(i, i ^ bit) for i in range(n)])


def after(value, *others):
    return lax.optimization_barrier((value, *others))[0]


def launch(value):
    far = swap(value, "row", 6)
    return [value, swap(value, "row", 2), swap(value, "row", 4), far]


def land(came, p, *others):
    n_row = lax.axis_size("row")
    came = lax.optimization_barrier((*came, *others))
    q = (p >> 1) & 3

    def pick(d):
        return jnp.where(d == 0, came[0], jnp.where(d == 1, came[1], jnp.where(d == 2, came[2], came[3])))

    near, far = pick(q), pick(q ^ 1)
    bit = 8
    while bit < n_row:
        near = jnp.where((p & bit) == 0, near, swap(near, "row", bit))
        far = jnp.where((p & bit) == 0, far, swap(far, "row", bit))
        bit *= 2
    return near, far


def steps_right(s, n_col):
    return [(k + s, k + s + 1) for k in range(PANELS) if k + s + 1 < n_col]


def along_col(own, right_block, c):
    n_row, n_col = lax.axis_size("row"), lax.axis_size("col")
    direct = n_col == PANELS + 1
    right, left, chips = [], [], [right_block]
    value = back = own
    for s in range(n_col - 2):
        came = [lax.ppermute(value, "col", steps_right(s, n_col))]
        if s < PANELS - 1:
            pairs = [(r * n_col + k - s, r * n_col + k - s - 1) for r in range(n_row) for k in range(s + 1, PANELS)]
            if direct and s == 0:
                pairs += [(r * n_col, r * n_col + n_col - 1) for r in (0, 2)]
            came.append(lax.ppermute(back, ("row", "col"), pairs))
            if s == 0:
                came += [swap(right_block, "row", 2), swap(right_block, "row", 4)]
            if s == 1:
                came.append(swap(chips[2], "row", 2))
            value, back, *more = lax.optimization_barrier(tuple(came))
            left.append(back)
            chips += more
        else:
            value = came[0]
        right.append(value)

    def pick(k):
        value = own
        for s, came in enumerate(right):
            value = jnp.where(c == k + 1 + s, came, value)
        for s, came in enumerate(left):
            value = jnp.where(c == k - 1 - s, came, value)
        return value

    def start_last(*others):
        return lax.ppermute(after(value, *others), "col", steps_right(n_col - 2, n_col))

    def finish(came, *others):
        return jnp.where(c == n_col - 1, after(came, *others), pick(0))

    if direct:
        ahead = jnp.where(c == n_col - 1, left[0], pick(0))
    else:
        ahead = finish(start_last())
    return ahead, [None, pick(1), pick(2)], chips, start_last, finish


def shards(kernel):
    n_col = lax.axis_size("col")
    p = lax.axis_index("row")
    c = lax.axis_index("col")
    nb = kernel.shape[1]
    core = p & 1
    chip = (p >> 1) & 3
    f32 = jnp.float32
    own = kernel[0, :, 0, :]
    right = kernel[0, :, 1, :]
    place = jnp.stack([p, c]).astype(jnp.int32)
    smem = pl.BlockSpec(memory_space=pltpu.SMEM)
    vmem = pl.BlockSpec(memory_space=pltpu.VMEM)
    square = jax.ShapeDtypeStruct((nb, nb), f32)
    chain = [pltpu.VMEM((nb, nb), f32)]

    def call(body, name, outs, scratch, micros, *operands):
        return pl.pallas_call(
            body,
            out_shape=outs,
            in_specs=[smem] + [vmem] * len(operands),
            out_specs=jax.tree.map(lambda _: vmem, outs),
            scratch_shapes=scratch,
            compiler_params=pltpu.CompilerParams(vmem_limit_bytes=24 * 1024 * 1024),
            cost_estimate=pl.CostEstimate(flops=0, bytes_accessed=int(micros * 3.5e6), transcendentals=0),
            name=name,
        )(place, *operands)

    def cut(blocks):
        parts = blocks.reshape(-1, 2, HALF, nb)
        kept = jnp.where(core == 0, parts[:, 0], parts[:, 1])
        got = swap(jnp.where(core == 0, parts[:, 1], parts[:, 0]), "row", 1)
        return jnp.where(core == 0, kept, got), jnp.where(core == 0, got, kept)

    def cross(*values):
        mine = jnp.concatenate(values)
        return [mine, swap(mine, "row", 1)]

    ahead, blocks, top, start_last, finish = along_col(own, right, c)
    even, odd = cut(jnp.stack([ahead, blocks[1], blocks[2]]))
    one = launch(even[0])
    two = launch(jnp.concatenate([even[1], jnp.where(chip == 0, odd[1], even[2])]))
    top = cross(*land(top, p))
    one = land(one, p, *top, *two[1:3])
    last = start_last(*one)
    one = cross(*one)
    w0 = call(first_kernel, "first", square, chain, 6.5, *one)
    blocks[0] = finish(last, w0)
    two = cross(*land(two, p, w0, blocks[0]))
    top_own = launch(after(own, w0))
    inverses, upper = call(
        rest_kernel, "rest",
        (jax.ShapeDtypeStruct((2, nb, nb), f32), jax.ShapeDtypeStruct((PANELS, nb, nb), f32)),
        [*chain, pltpu.VMEM((2, nb, nb), f32)], 15.0,
        w0, *one, *two)
    top_own = cross(*land(top_own, p, inverses))
    return call(
        apply_kernel, "apply", jax.ShapeDtypeStruct(kernel.shape, f32), [], 6.0,
        own, right, *blocks, w0, inverses, upper, *top, *top_own)


def solution(mesh):
    in_specs = (P(None, "row", None, "col"),)
    out_specs = P(None, "row", None, "col")
    return jax.shard_map(shards, mesh=mesh, in_specs=in_specs, out_specs=out_specs, check_vma=False)
```

```python
import jax
import jax.numpy as jnp
from jax import lax
from jax.experimental import pallas as pl
from jax.experimental.pallas import tpu as pltpu
from jax.sharding import PartitionSpec as P

PANELS = 3
HALF = 128
GROUPS = HALF // 8
NN = (((1,), (0,)), ((), ()))
NT = (((1,), (1,)), ((), ()))
TN = (((0,), (0,)), ((), ()))


def lane_b(x, j):
    return jnp.broadcast_to(x[:, j:j + 1], (8, 128))


def sub_b(x, t):
    return jnp.broadcast_to(x[t:t + 1, :], x.shape)


def wide(x):
    return jnp.concatenate([x, x], axis=1)


def split(x):
    high = x.astype(jnp.bfloat16)
    low = (x - high.astype(jnp.float32)).astype(jnp.bfloat16)
    return high, low


def mm(a, b, dims):
    dot = lambda u, v: lax.dot_general(u, v, dims, preferred_element_type=jnp.float32)
    return dot(a[0], b[0]) + (dot(a[0], b[1]) + dot(a[1], b[0]))


def eliminate(rows, shift):
    count = len(rows)
    iota = lax.broadcasted_iota(jnp.int32, (8, 128), 0)
    rows = list(rows)
    out = []
    ahead = None
    for b in range(count):
        k = shift + 8 * b
        cols = {g: [lane_b(rows[g], k + j) for j in range(8)] for g in range(b, count) if g > b or ahead is None}
        if ahead is not None:
            cols[b] = ahead
        ahead = None
        if b + 1 < count:
            ahead = [lane_b(rows[b + 1], k + 8 + j) for j in range(8)]
        da = jnp.ones((8, 128), jnp.float32)
        db = jnp.zeros((8, 128), jnp.float32)
        dc = jnp.ones((8, 128), jnp.float32)
        pp = jnp.zeros((8, 256), jnp.float32)
        for t in range(0, 8, 2):
            first = {j: sub_b(cols[b][j], t) for j in range(t, 8)}
            second = {j: sub_b(cols[b][j], t + 1) for j in range(t + 1, 8)}
            a, q, c = first[t], first[t + 1], second[t + 1]
            rd = 1.0 / (a * c - q * q)
            da = jnp.where((iota == t) | (iota == t + 1), a, da)
            db = jnp.where(iota == t + 1, q, db)
            dc = jnp.where(iota == t + 1, c, dc)
            p0, p1 = sub_b(rows[b], t), sub_b(rows[b], t + 1)
            pp = jnp.where(wide(iota == t + 1), p0, pp)
            for g in range(b, count):
                if g == b and t == 6:
                    continue
                c0, c1 = cols[g][t], cols[g][t + 1]
                n0, n1 = c0 * c - c1 * q, c1 * a - c0 * q
                if g == b:
                    n0 = jnp.where(iota > t + 1, n0, 0.0)
                    n1 = jnp.where(iota > t + 1, n1, 0.0)
                m0, m1 = n0 * rd, n1 * rd
                rows[g] = rows[g] - (wide(m0) * p0 + wide(m1) * p1)
                for j in range(t + 2, 8):
                    cols[g][j] = cols[g][j] - (m0 * first[j] + m1 * second[j])
                if g == b + 1:
                    for j in range(8):
                        ahead[j] = ahead[j] - (m0 * sub_b(c0, j) + m1 * sub_b(c1, j))
        odd = (iota % 2) == 1
        f = jnp.where(odd, db / da, 0.0)
        piv = jnp.where(odd, dc - db * f, da)
        out.append((rows[b] - wide(f) * pp) * wide(lax.rsqrt(piv)))
    return out


def factor_half(a):
    half = GROUPS // 2
    aug = jnp.concatenate([a, identity(HALF)], axis=1)
    upper = eliminate([aug[8 * g:8 * g + 8, :] for g in range(half)], 0)
    high, low = split(jnp.concatenate(upper, axis=0))
    left = jnp.concatenate([high[:, :HALF], high[:, :HALF], low[:, :HALF]], axis=0)
    right = jnp.concatenate([high, low, high], axis=0)
    update = lax.dot_general(left, right, TN, preferred_element_type=jnp.float32)
    under = eliminate(
        [aug[8 * g:8 * g + 8, :] - update[8 * g:8 * g + 8, :] for g in range(half, GROUPS)], HALF // 2)
    return jnp.concatenate(upper + under, axis=0)[:, HALF:]


def identity(n):
    r = lax.broadcasted_iota(jnp.int32, (n, n), 0)
    c = lax.broadcasted_iota(jnp.int32, (n, n), 1)
    return jnp.where(r == c, 1.0, 0.0).astype(jnp.float32)


def factor_panel(corner, side, rest, inverse):
    w0 = factor_half(corner)
    sw0 = split(w0)
    side = split(side)
    low = split(mm(side, sw0, NT))
    w1 = factor_half(rest - mm(low, split(mm(sw0, side, NT)), NN))
    inverse[:HALF, :HALF] = w0
    inverse[:HALF, HALF:] = jnp.zeros((HALF, HALF), jnp.float32)
    inverse[HALF:, :HALF] = -mm(split(w1), split(mm(low, sw0, NN)), NN)
    inverse[HALF:, HALF:] = w1


def quarters(block):
    return block[:HALF, :HALF], block[HALF:, :HALF], block[HALF:, HALF:]


def less_square(block, a, b):
    q00, q10, q11 = quarters(block)
    return q00 - mm(a, a, TN), q10 - mm(b, a, TN), q11 - mm(b, b, TN)


def halves(mine, other, core):
    a, b = mine[...], other[...]
    return jnp.concatenate([jnp.where(core == 0, a, b), jnp.where(core == 0, b, a)], axis=0)


def three(refs, core):
    near, far, near_other, far_other = refs
    return [
        jnp.where(core == 0, near[...], near_other[...]),
        jnp.where(core == 0, near_other[...], near[...]),
        jnp.where(core == 0, far[...], far_other[...]),
    ]


def first_kernel(place, mine_ref, other_ref, inverse_ref, block):
    block[...] = halves(mine_ref.at[:HALF], other_ref.at[:HALF], lax.rem(place[0], 2))
    factor_panel(*quarters(block[...]), inverse_ref)


def rest_kernel(place, w0_ref, *refs):
    pieces, inverses, upper = (refs[:2], refs[2:4]), refs[4], refs[5]
    core = lax.rem(place[0], 2)

    def piece(group, k):
        mine, other = pieces[group]
        return halves(mine.at[k * HALF:(k + 1) * HALF], other.at[k * HALF:(k + 1) * HALF], core)

    w0 = split(w0_ref[...])
    a01 = piece(1, 0)
    u01a = mm(w0, split(a01[:, :HALF]), NN)
    u01b = mm(w0, split(a01[:, HALF:]), NN)
    factor_panel(*less_square(piece(1, 1), split(u01a), split(u01b)), inverses.at[0])
    u01 = jnp.concatenate([u01a, u01b], axis=1)
    u02 = mm(w0, split(piece(0, 1)), NT)
    upper[0] = u01
    upper[1] = u02
    su01, su02 = split(u01), split(u02)
    s21 = piece(1, 2) - mm(su02, su01, TN)
    rest = piece(1, 3) - mm(su02, su02, TN)
    w1 = split(inverses[0])
    u12a = mm(w1, split(s21[:HALF]), NT)
    u12b = mm(w1, split(s21[HALF:]), NT)
    factor_panel(*less_square(rest, split(u12a), split(u12b)), inverses.at[1])
    upper[2] = jnp.concatenate([u12a, u12b], axis=1)


def apply_kernel(place, own_ref, right_ref, b0_ref, b1_ref, b2_ref, w0_ref, inverses, upper, *refs):
    top_refs, out_ref = (refs[2:4], refs[:2]), refs[4]
    p, c = place[0], place[1]
    core = lax.rem(p, 2)
    nb = 2 * HALF

    def blocks(members):
        w0, w1, w2 = [split(w) for w in (w0_ref[...], inverses[0], inverses[1])]
        u01, u02, u12 = [split(upper[k]) for k in range(PANELS)]
        x0 = mm(split(b0_ref[...]), w0, NT)
        if members:
            tops = [three([ref.at[k:k + nb] for ref in top_refs[member] for k in (0, nb)], core) for member in members]
            t0, t1, t2 = [jnp.concatenate(t, axis=1) for t in zip(*tops)]
            y0 = split(mm(w0, split(t0), NN))
        sx0 = split(x0)
        x1 = mm(split(b1_ref[...] - mm(sx0, u01, NN)), w1, NT)
        if members:
            y1 = split(mm(w1, split(t1 - mm(u01, y0, TN)), NN))
        sx1 = split(x1)
        x2 = mm(split(b2_ref[...] - mm(sx0, u02, NN) - mm(sx1, u12, NN)), w2, NT)
        if members:
            y2 = split(mm(w2, split(t2 - mm(u02, y0, TN) - mm(u12, y1, TN)), NN))
            row = tuple(jnp.concatenate(parts, axis=1) for parts in zip(sx0, sx1, split(x2)))
            column = tuple(jnp.concatenate(parts, axis=0) for parts in zip(y0, y1, y2))
            loss = mm(row, column, NN)
            for i, member in enumerate(members):
                out_ref[0, :, member, :] = (own_ref, right_ref)[member][...] - loss[:, i * nb:(i + 1) * nb]
        return x0, x1, x2

    def panel(x0, x1, x2):
        r = lax.broadcasted_iota(jnp.int32, (nb, nb), 0)
        q = lax.broadcasted_iota(jnp.int32, (nb, nb), 1)
        keep = jnp.where(p > c, 1, 0)
        diagonal = jnp.where(p == c, 1, 0)
        mask = (keep + diagonal * jnp.where(r >= q, 1, 0)) > 0
        value = jnp.where(c == 0, x0, jnp.where(c == 1, x1, x2))
        out_ref[0, :, 0, :] = jnp.where(mask, value, 0.0)

    @pl.when((p >= PANELS) & (c >= PANELS))
    def _():
        blocks((0, 1))

    @pl.when((p >= PANELS) & (c < PANELS))
    def _():
        panel(*blocks((1,)))

    @pl.when((p < PANELS) & (c < PANELS))
    def _():
        panel(*blocks(()))
        out_ref[0, :, 1, :] = jnp.zeros((nb, nb), jnp.float32)

    @pl.when((p < PANELS) & (c >= PANELS))
    def _():
        out_ref[0, :, 0, :] = jnp.zeros((nb, nb), jnp.float32)
        out_ref[0, :, 1, :] = jnp.zeros((nb, nb), jnp.float32)


def swap(value, axis, bit):
    n = lax.axis_size(axis)
    return lax.ppermute(value, axis, [(i, i ^ bit) for i in range(n)])


def after(value, *others):
    return lax.optimization_barrier((value, *others))[0]


def launch(value):
    far = swap(value, "row", 6)
    return [value, swap(value, "row", 2), swap(value, "row", 4), far]


def land(came, p, *others):
    n_row = lax.axis_size("row")
    came = lax.optimization_barrier((*came, *others))
    q = (p >> 1) & 3

    def pick(d):
        return jnp.where(d == 0, came[0], jnp.where(d == 1, came[1], jnp.where(d == 2, came[2], came[3])))

    near, far = pick(q), pick(q ^ 1)
    bit = 8
    while bit < n_row:
        near = jnp.where((p & bit) == 0, near, swap(near, "row", bit))
        far = jnp.where((p & bit) == 0, far, swap(far, "row", bit))
        bit *= 2
    return near, far


def steps_right(s, n_col):
    return [(k + s, k + s + 1) for k in range(PANELS) if k + s + 1 < n_col]


def along_col(own, right_block, c):
    n_row, n_col = lax.axis_size("row"), lax.axis_size("col")
    direct = n_col == PANELS + 1
    right, left, chips = [], [], [right_block]
    value = back = own
    for s in range(n_col - 2):
        came = [lax.ppermute(value, "col", steps_right(s, n_col))]
        if s < PANELS - 1:
            pairs = [(r * n_col + k - s, r * n_col + k - s - 1) for r in range(n_row) for k in range(s + 1, PANELS)]
            if direct and s == 0:
                pairs += [(r * n_col, r * n_col + n_col - 1) for r in (0, 2)]
            came.append(lax.ppermute(back, ("row", "col"), pairs))
            if s == 0:
                came += [swap(right_block, "row", 2), swap(right_block, "row", 4)]
            if s == 1:
                came.append(swap(chips[2], "row", 2))
            value, back, *more = lax.optimization_barrier(tuple(came))
            left.append(back)
            chips += more
        else:
            value = came[0]
        right.append(value)

    def pick(k):
        value = own
        for s, came in enumerate(right):
            value = jnp.where(c == k + 1 + s, came, value)
        for s, came in enumerate(left):
            value = jnp.where(c == k - 1 - s, came, value)
        return value

    def start_last(*others):
        return lax.ppermute(after(value, *others), "col", steps_right(n_col - 2, n_col))

    def finish(came, *others):
        return jnp.where(c == n_col - 1, after(came, *others), pick(0))

    if direct:
        ahead = jnp.where(c == n_col - 1, left[0], pick(0))
    else:
        ahead = finish(start_last())
    return ahead, [None, pick(1), pick(2)], chips, start_last, finish


def shards(kernel):
    n_col = lax.axis_size("col")
    p = lax.axis_index("row")
    c = lax.axis_index("col")
    nb = kernel.shape[1]
    core = p & 1
    chip = (p >> 1) & 3
    f32 = jnp.float32
    own = kernel[0, :, 0, :]
    right = kernel[0, :, 1, :]
    place = jnp.stack([p, c]).astype(jnp.int32)
    smem = pl.BlockSpec(memory_space=pltpu.SMEM)
    vmem = pl.BlockSpec(memory_space=pltpu.VMEM)
    square = jax.ShapeDtypeStruct((nb, nb), f32)
    chain = [pltpu.VMEM((nb, nb), f32)]

    def call(body, name, outs, scratch, micros, *operands):
        return pl.pallas_call(
            body,
            out_shape=outs,
            in_specs=[smem] + [vmem] * len(operands),
            out_specs=jax.tree.map(lambda _: vmem, outs),
            scratch_shapes=scratch,
            compiler_params=pltpu.CompilerParams(vmem_limit_bytes=24 * 1024 * 1024),
            cost_estimate=pl.CostEstimate(flops=0, bytes_accessed=int(micros * 3.5e6), transcendentals=0),
            name=name,
        )(place, *operands)

    def cut(blocks):
        parts = blocks.reshape(-1, 2, HALF, nb)
        kept = jnp.where(core == 0, parts[:, 0], parts[:, 1])
        got = swap(jnp.where(core == 0, parts[:, 1], parts[:, 0]), "row", 1)
        return jnp.where(core == 0, kept, got), jnp.where(core == 0, got, kept)

    def cross(*values):
        mine = jnp.concatenate(values)
        return [mine, swap(mine, "row", 1)]

    ahead, blocks, top, start_last, finish = along_col(own, right, c)
    even, odd = cut(jnp.stack([ahead, blocks[1], blocks[2]]))
    one = launch(even[0])
    two = launch(jnp.concatenate([even[1], jnp.where(chip == 0, odd[1], even[2])]))
    top = cross(*land(top, p))
    one = land(one, p, *top, *two[1:3])
    last = start_last(*one)
    one = cross(*one)
    w0 = call(first_kernel, "first", square, chain, 6.5, *one)
    blocks[0] = finish(last, w0)
    two = cross(*land(two, p, w0, blocks[0]))
    top_own = launch(after(own, w0))
    inverses, upper = call(
        rest_kernel, "rest",
        (jax.ShapeDtypeStruct((2, nb, nb), f32), jax.ShapeDtypeStruct((PANELS, nb, nb), f32)),
        [], 15.0,
        w0, *one, *two)
    top_own = cross(*land(top_own, p, inverses))
    return call(
        apply_kernel, "apply", jax.ShapeDtypeStruct(kernel.shape, f32), [], 6.0,
        own, right, *blocks, w0, inverses, upper, *top, *top_own)


def solution(mesh):
    in_specs = (P(None, "row", None, "col"),)
    out_specs = P(None, "row", None, "col")
    return jax.shard_map(shards, mesh=mesh, in_specs=in_specs, out_specs=out_specs, check_vma=False)
```

```python
import jax
import jax.numpy as jnp
from jax import lax
from jax.experimental import pallas as pl
from jax.experimental.pallas import tpu as pltpu
from jax.sharding import PartitionSpec as P

PANELS = 3
HALF = 128
GROUPS = HALF // 8
NN = (((1,), (0,)), ((), ()))
NT = (((1,), (1,)), ((), ()))
TN = (((0,), (0,)), ((), ()))


def lane_b(x, j):
    return jnp.broadcast_to(x[:, j:j + 1], (8, 128))


def sub_b(x, t):
    return jnp.broadcast_to(x[t:t + 1, :], x.shape)


def wide(x):
    return jnp.concatenate([x, x], axis=1)


def split(x):
    high = x.astype(jnp.bfloat16)
    low = (x - high.astype(jnp.float32)).astype(jnp.bfloat16)
    return high, low


def mm(a, b, dims):
    dot = lambda u, v: lax.dot_general(u, v, dims, preferred_element_type=jnp.float32)
    return dot(a[0], b[0]) + (dot(a[0], b[1]) + dot(a[1], b[0]))


def eliminate(rows, shift):
    count = len(rows)
    iota = lax.broadcasted_iota(jnp.int32, (8, 128), 0)
    rows = list(rows)
    out = []
    ahead = None
    for b in range(count):
        k = shift + 8 * b
        cols = {g: [lane_b(rows[g], k + j) for j in range(8)] for g in range(b, count) if g > b or ahead is None}
        if ahead is not None:
            cols[b] = ahead
        ahead = None
        if b + 1 < count:
            ahead = [lane_b(rows[b + 1], k + 8 + j) for j in range(8)]
        da = jnp.ones((8, 128), jnp.float32)
        db = jnp.zeros((8, 128), jnp.float32)
        dc = jnp.ones((8, 128), jnp.float32)
        pp = jnp.zeros((8, 256), jnp.float32)
        for t in range(0, 8, 2):
            first = {j: sub_b(cols[b][j], t) for j in range(t, 8)}
            second = {j: sub_b(cols[b][j], t + 1) for j in range(t + 1, 8)}
            a, q, c = first[t], first[t + 1], second[t + 1]
            rd = 1.0 / (a * c - q * q)
            da = jnp.where((iota == t) | (iota == t + 1), a, da)
            db = jnp.where(iota == t + 1, q, db)
            dc = jnp.where(iota == t + 1, c, dc)
            p0, p1 = sub_b(rows[b], t), sub_b(rows[b], t + 1)
            pp = jnp.where(wide(iota == t + 1), p0, pp)
            for g in range(b, count):
                if g == b and t == 6:
                    continue
                c0, c1 = cols[g][t], cols[g][t + 1]
                n0, n1 = c0 * c - c1 * q, c1 * a - c0 * q
                if g == b:
                    n0 = jnp.where(iota > t + 1, n0, 0.0)
                    n1 = jnp.where(iota > t + 1, n1, 0.0)
                m0, m1 = n0 * rd, n1 * rd
                rows[g] = rows[g] - (wide(m0) * p0 + wide(m1) * p1)
                for j in range(t + 2, 8):
                    cols[g][j] = cols[g][j] - (m0 * first[j] + m1 * second[j])
                if g == b + 1:
                    for j in range(8):
                        ahead[j] = ahead[j] - (m0 * sub_b(c0, j) + m1 * sub_b(c1, j))
        odd = (iota % 2) == 1
        f = jnp.where(odd, db / da, 0.0)
        piv = jnp.where(odd, dc - db * f, da)
        out.append((rows[b] - wide(f) * pp) * wide(lax.rsqrt(piv)))
    return out


def factor_half(a):
    half = GROUPS // 2
    aug = jnp.concatenate([a, identity(HALF)], axis=1)
    upper = eliminate([aug[8 * g:8 * g + 8, :] for g in range(half)], 0)
    high, low = split(jnp.concatenate(upper, axis=0))
    left = jnp.concatenate([high[:, :HALF], high[:, :HALF], low[:, :HALF]], axis=0)
    right = jnp.concatenate([high, low, high], axis=0)
    update = lax.dot_general(left, right, TN, preferred_element_type=jnp.float32)
    under = eliminate(
        [aug[8 * g:8 * g + 8, :] - update[8 * g:8 * g + 8, :] for g in range(half, GROUPS)], HALF // 2)
    return jnp.concatenate(upper + under, axis=0)[:, HALF:]


def identity(n):
    r = lax.broadcasted_iota(jnp.int32, (n, n), 0)
    c = lax.broadcasted_iota(jnp.int32, (n, n), 1)
    return jnp.where(r == c, 1.0, 0.0).astype(jnp.float32)


def factor_panel(corner, side, rest, inverse):
    w0 = factor_half(corner)
    sw0 = split(w0)
    side = split(side)
    low = split(mm(side, sw0, NT))
    w1 = factor_half(rest - mm(low, split(mm(sw0, side, NT)), NN))
    inverse[:HALF, :HALF] = w0
    inverse[:HALF, HALF:] = jnp.zeros((HALF, HALF), jnp.float32)
    inverse[HALF:, :HALF] = -mm(split(w1), split(mm(low, sw0, NN)), NN)
    inverse[HALF:, HALF:] = w1


def quarters(block):
    return block[:HALF, :HALF], block[HALF:, :HALF], block[HALF:, HALF:]


def less_square(block, a, b):
    q00, q10, q11 = quarters(block)
    return q00 - mm(a, a, TN), q10 - mm(b, a, TN), q11 - mm(b, b, TN)


def halves(mine, other, core):
    a, b = mine[...], other[...]
    return jnp.concatenate([jnp.where(core == 0, a, b), jnp.where(core == 0, b, a)], axis=0)


def three(refs, core):
    near, far, near_other, far_other = refs
    return [
        jnp.where(core == 0, near[...], near_other[...]),
        jnp.where(core == 0, near_other[...], near[...]),
        jnp.where(core == 0, far[...], far_other[...]),
    ]


def first_kernel(place, mine_ref, other_ref, inverse_ref, block):
    block[...] = halves(mine_ref.at[:HALF], other_ref.at[:HALF], lax.rem(place[0], 2))
    factor_panel(*quarters(block[...]), inverse_ref)


def rest_kernel(place, w0_ref, *refs):
    pieces, inverses, upper = (refs[:2], refs[2:4]), refs[4], refs[5]
    core = lax.rem(place[0], 2)

    def piece(group, k):
        mine, other = pieces[group]
        return halves(mine.at[k * HALF:(k + 1) * HALF], other.at[k * HALF:(k + 1) * HALF], core)

    w0 = split(w0_ref[...])
    a01 = piece(1, 0)
    u01a = mm(w0, split(a01[:, :HALF]), NN)
    u01b = mm(w0, split(a01[:, HALF:]), NN)
    factor_panel(*less_square(piece(1, 1), split(u01a), split(u01b)), inverses.at[0])
    u01 = jnp.concatenate([u01a, u01b], axis=1)
    u02 = mm(w0, split(piece(0, 1)), NT)
    upper[0] = u01
    upper[1] = u02
    su01, su02 = split(u01), split(u02)
    s21 = piece(1, 2) - mm(su02, su01, TN)
    rest = piece(1, 3) - mm(su02, su02, TN)
    w1 = split(inverses[0])
    u12a = mm(w1, split(s21[:HALF]), NT)
    u12b = mm(w1, split(s21[HALF:]), NT)
    factor_panel(*less_square(rest, split(u12a), split(u12b)), inverses.at[1])
    upper[2] = jnp.concatenate([u12a, u12b], axis=1)


def apply_kernel(place, own_ref, right_ref, b0_ref, b1_ref, b2_ref, w0_ref, inverses, upper, *refs):
    top_refs, out_ref = (refs[2:4], refs[:2]), refs[4]
    p, c = place[0], place[1]
    core = lax.rem(p, 2)
    nb = 2 * HALF

    def blocks(members):
        w0, w1, w2 = [split(w) for w in (w0_ref[...], inverses[0], inverses[1])]
        u01, u02, u12 = [split(upper[k]) for k in range(PANELS)]
        x0 = mm(split(b0_ref[...]), w0, NT)
        if members:
            tops = [three([ref.at[k:k + nb] for ref in top_refs[member] for k in (0, nb)], core) for member in members]
            t0, t1, t2 = [jnp.concatenate(t, axis=1) for t in zip(*tops)]
            y0 = split(mm(w0, split(t0), NN))
        sx0 = split(x0)
        x1 = mm(split(b1_ref[...] - mm(sx0, u01, NN)), w1, NT)
        if members:
            y1 = split(mm(w1, split(t1 - mm(u01, y0, TN)), NN))
        sx1 = split(x1)
        x2 = mm(split(b2_ref[...] - mm(sx0, u02, NN) - mm(sx1, u12, NN)), w2, NT)
        if members:
            y2 = split(mm(w2, split(t2 - mm(u02, y0, TN) - mm(u12, y1, TN)), NN))
            row = tuple(jnp.concatenate(parts, axis=1) for parts in zip(sx0, sx1, split(x2)))
            column = tuple(jnp.concatenate(parts, axis=0) for parts in zip(y0, y1, y2))
            loss = mm(row, column, NN)
            for i, member in enumerate(members):
                out_ref[0, :, member, :] = (own_ref, right_ref)[member][...] - loss[:, i * nb:(i + 1) * nb]
        return x0, x1, x2

    def panel(x0, x1, x2):
        r = lax.broadcasted_iota(jnp.int32, (nb, nb), 0)
        q = lax.broadcasted_iota(jnp.int32, (nb, nb), 1)
        keep = jnp.where(p > c, 1, 0)
        diagonal = jnp.where(p == c, 1, 0)
        mask = (keep + diagonal * jnp.where(r >= q, 1, 0)) > 0
        value = jnp.where(c == 0, x0, jnp.where(c == 1, x1, x2))
        out_ref[0, :, 0, :] = jnp.where(mask, value, 0.0)

    @pl.when((p >= PANELS) & (c >= PANELS))
    def _():
        blocks((0, 1))

    @pl.when((p >= PANELS) & (c < PANELS))
    def _():
        panel(*blocks((1,)))

    @pl.when((p < PANELS) & (c < PANELS))
    def _():
        panel(*blocks(()))
        out_ref[0, :, 1, :] = jnp.zeros((nb, nb), jnp.float32)

    @pl.when((p < PANELS) & (c >= PANELS))
    def _():
        out_ref[0, :, 0, :] = jnp.zeros((nb, nb), jnp.float32)
        out_ref[0, :, 1, :] = jnp.zeros((nb, nb), jnp.float32)


def swap(value, axis, bit):
    n = lax.axis_size(axis)
    return lax.ppermute(value, axis, [(i, i ^ bit) for i in range(n)])


def after(value, *others):
    return lax.optimization_barrier((value, *others))[0]


def launch(value):
    far = swap(value, "row", 6)
    return [value, swap(value, "row", 2), swap(value, "row", 4), far]


def launch_beyond(value):
    n_row, n_col = lax.axis_size("row"), lax.axis_size("col")
    far, x, y = [
        lax.ppermute(value, ("row", "col"), [
            (r * n_col + k, (r ^ bit) * n_col + k) for r in range(n_row) for k in range(PANELS, n_col)])
        for bit in (6, 2, 4)]
    return [value, x, y, far]


def land(came, p, *others):
    n_row = lax.axis_size("row")
    came = lax.optimization_barrier((*came, *others))
    q = (p >> 1) & 3

    def pick(d):
        return jnp.where(d == 0, came[0], jnp.where(d == 1, came[1], jnp.where(d == 2, came[2], came[3])))

    near, far = pick(q), pick(q ^ 1)
    bit = 8
    while bit < n_row:
        near = jnp.where((p & bit) == 0, near, swap(near, "row", bit))
        far = jnp.where((p & bit) == 0, far, swap(far, "row", bit))
        bit *= 2
    return near, far


def steps_right(s, n_col):
    return [(k + s, k + s + 1) for k in range(PANELS) if k + s + 1 < n_col]


def along_col(own, right_block, c):
    n_row, n_col = lax.axis_size("row"), lax.axis_size("col")
    direct = n_col == PANELS + 1
    right, left, chips = [], [], [right_block]
    value = back = own
    for s in range(n_col - 2):
        came = [lax.ppermute(value, "col", steps_right(s, n_col))]
        if s < PANELS - 1:
            pairs = [(r * n_col + k - s, r * n_col + k - s - 1) for r in range(n_row) for k in range(s + 1, PANELS)]
            if direct and s == 0:
                pairs += [(r * n_col, r * n_col + n_col - 1) for r in (0, 2)]
            came.append(lax.ppermute(back, ("row", "col"), pairs))
            if s == 0:
                came += [swap(right_block, "row", 2), swap(right_block, "row", 4)]
            if s == 1:
                came.append(swap(chips[2], "row", 2))
            value, back, *more = lax.optimization_barrier(tuple(came))
            left.append(back)
            chips += more
        else:
            value = came[0]
        right.append(value)

    def pick(k):
        value = own
        for s, came in enumerate(right):
            value = jnp.where(c == k + 1 + s, came, value)
        for s, came in enumerate(left):
            value = jnp.where(c == k - 1 - s, came, value)
        return value

    def start_last(*others):
        return lax.ppermute(after(value, *others), "col", steps_right(n_col - 2, n_col))

    def finish(came, *others):
        return jnp.where(c == n_col - 1, after(came, *others), pick(0))

    if direct:
        ahead = jnp.where(c == n_col - 1, left[0], pick(0))
    else:
        ahead = finish(start_last())
    return ahead, [None, pick(1), pick(2)], chips, start_last, finish


def shards(kernel):
    n_col = lax.axis_size("col")
    p = lax.axis_index("row")
    c = lax.axis_index("col")
    nb = kernel.shape[1]
    core = p & 1
    chip = (p >> 1) & 3
    f32 = jnp.float32
    own = kernel[0, :, 0, :]
    right = kernel[0, :, 1, :]
    place = jnp.stack([p, c]).astype(jnp.int32)
    smem = pl.BlockSpec(memory_space=pltpu.SMEM)
    vmem = pl.BlockSpec(memory_space=pltpu.VMEM)
    square = jax.ShapeDtypeStruct((nb, nb), f32)
    chain = [pltpu.VMEM((nb, nb), f32)]

    def call(body, name, outs, scratch, micros, *operands):
        return pl.pallas_call(
            body,
            out_shape=outs,
            in_specs=[smem] + [vmem] * len(operands),
            out_specs=jax.tree.map(lambda _: vmem, outs),
            scratch_shapes=scratch,
            compiler_params=pltpu.CompilerParams(vmem_limit_bytes=24 * 1024 * 1024),
            cost_estimate=pl.CostEstimate(flops=0, bytes_accessed=int(micros * 3.5e6), transcendentals=0),
            name=name,
        )(place, *operands)

    def cut(blocks):
        parts = blocks.reshape(-1, 2, HALF, nb)
        kept = jnp.where(core == 0, parts[:, 0], parts[:, 1])
        got = swap(jnp.where(core == 0, parts[:, 1], parts[:, 0]), "row", 1)
        return jnp.where(core == 0, kept, got), jnp.where(core == 0, got, kept)

    def cross(*values):
        mine = jnp.concatenate(values)
        return [mine, swap(mine, "row", 1)]

    ahead, blocks, top, start_last, finish = along_col(own, right, c)
    even, odd = cut(jnp.stack([ahead, blocks[1], blocks[2]]))
    one = launch(even[0])
    two = launch(jnp.concatenate([even[1], jnp.where(chip == 0, odd[1], even[2])]))
    top = cross(*land(top, p))
    one = land(one, p, *top, *two[1:3])
    last = start_last(*one)
    one = cross(*one)
    w0 = call(first_kernel, "first", square, chain, 6.5, *one)
    blocks[0] = finish(last, w0)
    two = cross(*land(two, p, w0, blocks[0]))
    top_own = launch_beyond(after(own, w0))
    inverses, upper = call(
        rest_kernel, "rest",
        (jax.ShapeDtypeStruct((2, nb, nb), f32), jax.ShapeDtypeStruct((PANELS, nb, nb), f32)),
        [], 15.0,
        w0, *one, *two)
    top_own = cross(*land(top_own, p, inverses))
    return call(
        apply_kernel, "apply", jax.ShapeDtypeStruct(kernel.shape, f32), [], 6.0,
        own, right, *blocks, w0, inverses, upper, *top, *top_own)


def solution(mesh):
    in_specs = (P(None, "row", None, "col"),)
    out_specs = P(None, "row", None, "col")
    return jax.shard_map(shards, mesh=mesh, in_specs=in_specs, out_specs=out_specs, check_vma=False)
```
